512 devices in a mesh: segment: 2 (over core), expert: 64 (over y, z), pair: 4 (over x).
Axes of the slice: x: 4, y: 4, z: 16, core: 2. Of those that a mesh axis runs over, the one named last changes fastest.
Arguments:
- acts: bfloat16 [2, 2, 12288, 768], P(None, None, 'expert', 'pair'), may hold values from -20 to 20
- cotangent: bfloat16 [2, 12288, 768], P(None, 'expert', 'pair'), may hold values from -6 to 6
- gates: float32 [2, 2, 12288], P(None, None, 'expert'), may hold values from 0.2 to 1
- owners: int32 [2, 2, 12288], P(None, None, 'expert'), may hold values from 0 to 63, as said below
- slots: int32 [2, 2, 12288], P(None, None, 'expert'), may hold values from 0 to 3
- w_in: bfloat16 [2, 64, 768, 3072], P('segment', 'expert', None, 'pair'), may hold values from -0.21875 to 0.21875
- w_out: bfloat16 [2, 64, 3072, 768], P('segment', 'expert', 'pair'), may hold values from -0.109375 to 0.109375
Outputs:
- grads: bfloat16 [2, 2, 12288, 768], P('segment', None, 'expert', 'pair')
- grad_in: bfloat16 [2, 64, 768, 3072], P('segment', 'expert', None, 'pair')
- grad_out: bfloat16 [2, 64, 3072, 768], P('segment', 'expert', 'pair')
The draws below stay inside these ranges and needn't reach their ends.
Inputs may be any that keep to these rules, and one draw needn't show every extreme that they name: `owners`: within each aligned block of 192 tokens of one sublayer and micro-batch, no two tokens share both owner and slot. One expert, the same for all blocks of a draw, takes exactly 4 tokens of every block.
All inputs are finite; a program needn't handle non-finite values.
Results may differ from the reference program's by a relative error of at most 0.02.
Values may be sent and summed in bfloat16 or wider, within the bound.
No kernel may reach another device: no remote copies, remote signals or barrier semaphores. Data moves between devices by JAX's collectives and lax.ppermute only.
A program may use at most 64 MiB of HBM per device.

```python
import math
import jax
import jax.numpy as jnp
from jax import lax

D = 768
FF = 3072
TOK_DEV = 192
MICRO = 2
EXPERTS = 64
CAP = 4
TOKENS = 12288
N_PAIR = 4


def routing(key):
    block_count = 2 * MICRO * (TOKENS // TOK_DEV)
    keys = jax.random.split(key, block_count + 1)
    favored = jax.random.randint(keys[0], (), 0, EXPERTS).astype(jnp.int32)

    def one_block(block_key):
        first_key, second_key = jax.random.split(block_key)
        chosen = jax.random.permutation(first_key, (EXPERTS - 1) * CAP)[:TOK_DEV - CAP].astype(jnp.int32)
        others = chosen // CAP
        owner_part = others + (others >= favored).astype(jnp.int32)
        slot_part = chosen % CAP
        owner_all = jnp.concatenate([jnp.full((CAP,), favored, jnp.int32), owner_part])
        slot_all = jnp.concatenate([jnp.arange(CAP, dtype=jnp.int32), slot_part])
        order = jax.random.permutation(second_key, TOK_DEV)
        return (owner_all[order], slot_all[order])
    owner_blocks, slot_blocks = jax.vmap(one_block)(keys[1:])
    return (owner_blocks.reshape(2, MICRO, TOKENS).astype(jnp.int32), slot_blocks.reshape(2, MICRO, TOKENS).astype(jnp.int32))


def draw_owners(key, part):
    return routing(key)[0]


def draw_slots(key, part):
    return routing(key)[1]


def draw_acts(key, part):
    key = jax.random.fold_in(key, 7)
    base_key, row_key, col_key = jax.random.split(key, 3)
    shape = (2, MICRO, TOKENS, D)
    row_scale = jnp.exp(jax.random.uniform(row_key, (2, MICRO, TOKENS, 1), jnp.float32, 0.0, math.log(10.0)))
    col_scale = jnp.exp(jax.random.uniform(col_key, (2, 1, 1, D), jnp.float32, 0.0, math.log(10.0)))
    base = jax.random.normal(base_key, shape, jnp.float32)
    base = jnp.clip(base, -4.0, 4.0)
    return (base * row_scale * col_scale / 20.0).astype(jnp.bfloat16)


def block_scale(key, dims, cuts, least, largest):
    level = 1.0
    for dim, blocks in cuts:
        steps = jax.random.uniform(jax.random.fold_in(jax.random.fold_in(key, 6), dim), (blocks,), jnp.float32, least / len(cuts), largest / len(cuts))
        level = level * jnp.repeat(jnp.exp(steps), dims[dim] // blocks).reshape((-1,) + (1,) * (len(dims) - 1 - dim))
    return level


def normal_values(stream_key, extent, spread, most, cuts=(), kind=jnp.bfloat16):
    factor_of = block_scale(stream_key, extent, cuts, -0.22, 0.18) if cuts else 1.0
    values = jax.random.normal(stream_key, extent, jnp.float32) * spread * factor_of
    return jnp.minimum(jnp.maximum(values, -most), most).astype(kind)


def setup_inputs(seed: int = 0) -> dict:
    key_list = jax.random.split(jax.random.key(seed), 8)
    return {
        "acts": draw_acts(jax.random.fold_in(key_list[7], 71), 0),
        "cotangent": normal_values(key_list[1], (MICRO, TOKENS, D), 1.0, 6.0, ((1, 64), (2, 4))),
        "gates": jnp.clip(0.2 + 0.8 * jax.random.uniform(key_list[2], (2, MICRO, TOKENS), jnp.float32) ** block_scale(key_list[2], (2, MICRO, TOKENS), ((2, 64),), -0.2, 0.2), 0.2, 1.0),
        "owners": draw_owners(jax.random.fold_in(key_list[7], 71), 0),
        "slots": draw_slots(jax.random.fold_in(key_list[7], 71), 0),
        "w_in": normal_values(key_list[5], (2, EXPERTS, D, FF), D ** -0.5, 0.21875, ((0, 2), (1, 64), (3, 4))),
        "w_out": normal_values(key_list[6], (2, EXPERTS, FF, D), FF ** -0.5, 0.109375, ((0, 2), (1, 64), (2, 4))),
    }


def gelu_value(pre_act):
    inner_arg = 0.7978845608 * (pre_act + 0.044715 * pre_act * pre_act * pre_act)
    return 0.5 * pre_act * (1.0 + jnp.tanh(inner_arg))

def gelu_slope(pre_act):
    inner_arg = 0.7978845608 * (pre_act + 0.044715 * pre_act * pre_act * pre_act)
    tangent = jnp.tanh(inner_arg)
    return 0.5 * (1.0 + tangent) + 0.5 * pre_act * (1.0 - tangent * tangent) * 0.7978845608 * (1.0 + 0.134145 * pre_act * pre_act)

def layer_reference(layer_acts, upstream, gate_row, owner_row, slot_row, first_weights, second_weights):
    act_float = layer_acts.astype(jnp.float32)
    scale_inv = lax.rsqrt(lax.optimization_barrier(jnp.mean(act_float * act_float, axis=1)) + 1e-06)
    normed = (act_float * scale_inv[:, None]).astype(jnp.bfloat16)
    scaled = (gate_row[:, None] * upstream.astype(jnp.float32)).astype(jnp.bfloat16)
    source_block = (jnp.arange(TOKENS) // TOK_DEV).astype(jnp.int32)
    position = source_block * CAP + slot_row.astype(jnp.int32)
    slot_total = TOKENS // TOK_DEV * CAP
    expert_in = jnp.zeros((EXPERTS, slot_total, D), jnp.bfloat16).at[owner_row, position].set(normed)
    expert_grad = jnp.zeros((EXPERTS, slot_total, D), jnp.bfloat16).at[owner_row, position].set(scaled)
    block_count = 2 * N_PAIR

    def per_expert(operands):
        rows_in, rows_grad, weight_first, weight_second = operands
        pre_act = jnp.dot(rows_in, weight_first, preferred_element_type=jnp.float32)
        hidden = gelu_value(pre_act).astype(jnp.bfloat16)
        back_hidden = jnp.dot(rows_grad, weight_second.T, preferred_element_type=jnp.float32)
        back_pre = (back_hidden * gelu_slope(pre_act)).astype(jnp.bfloat16)
        grad_first = jnp.dot(rows_in.T, back_pre, preferred_element_type=jnp.float32)
        grad_second = jnp.dot(hidden.T, rows_grad, preferred_element_type=jnp.float32)
        blocks = back_pre.astype(jnp.float32).reshape(slot_total, block_count, FF // block_count)
        weight_blocks = weight_first.astype(jnp.float32).reshape(D, block_count, FF // block_count)
        partials = jnp.einsum('rpf,dpf->prd', blocks, weight_blocks)
        summed = lax.optimization_barrier(jnp.sum(partials.astype(jnp.bfloat16).astype(jnp.float32), axis=0))
        return (grad_first, grad_second, summed)
    grad_first, grad_second, summed = lax.map(per_expert, (expert_in, expert_grad, first_weights, second_weights))
    arrived = summed[owner_row, position]
    inner = lax.optimization_barrier(jnp.sum(arrived * act_float, axis=1))
    branch = (scale_inv[:, None] * arrived - (scale_inv ** 3 * inner / D)[:, None] * act_float).astype(jnp.bfloat16)
    result = (upstream.astype(jnp.float32) + branch.astype(jnp.float32)).astype(jnp.bfloat16)
    return (result, grad_first, grad_second)

def reference(acts, cotangent, gates, owners, slots, w_in, w_out):
    upper_list = []
    lower_list = []
    upper_first = jnp.zeros((EXPERTS, D, FF), jnp.float32)
    upper_second = jnp.zeros((EXPERTS, FF, D), jnp.float32)
    lower_first = jnp.zeros((EXPERTS, D, FF), jnp.float32)
    lower_second = jnp.zeros((EXPERTS, FF, D), jnp.float32)
    for micro_index in range(MICRO):
        upper, first_term, second_term = layer_reference(acts[1, micro_index], cotangent[micro_index], gates[1, micro_index], owners[1, micro_index], slots[1, micro_index], w_in[1], w_out[1])
        upper_first = upper_first + first_term
        upper_second = upper_second + second_term
        lower, first_term, second_term = layer_reference(acts[0, micro_index], upper, gates[0, micro_index], owners[0, micro_index], slots[0, micro_index], w_in[0], w_out[0])
        lower_first = lower_first + first_term
        lower_second = lower_second + second_term
        upper_list.append(upper)
        lower_list.append(lower)
    grads = jnp.stack([jnp.stack(lower_list), jnp.stack(upper_list)])
    grad_in = jnp.stack([lower_first, upper_first]).astype(jnp.bfloat16)
    grad_out = jnp.stack([lower_second, upper_second]).astype(jnp.bfloat16)
    return (grads, grad_in, grad_out)
```

```python
import jax
import jax.numpy as jnp
from jax import lax
from jax.sharding import PartitionSpec as P

BF = jnp.bfloat16
F32 = jnp.float32
SWAP = [(0, 1), (1, 0)]


def gelu_both(u):
    s = jnp.tanh(0.7978845608 * (u + 0.044715 * u * u * u))
    value = 0.5 * u * (1.0 + s)
    slope = 0.5 * (1.0 + s) + 0.5 * u * (1.0 - s * s) * 0.7978845608 * (1.0 + 0.134145 * u * u)
    return value, slope


def dot(a, b, ca, cb):
    return lax.dot_general(a, b, (((ca,), (cb,)), ((), ())), preferred_element_type=F32)


def one_hot(owner, slot, rows, cap):
    target = owner * cap + slot
    return (lax.broadcasted_iota(jnp.int32, (rows, target.shape[0]), 0) == target[None, :]).astype(BF)


def expert_a2a(x):
    return lax.all_to_all(x, "expert", split_axis=0, concat_axis=0, tiled=True)


def pair_a2a(x):
    return lax.all_to_all(x, "pair", split_axis=0, concat_axis=0, tiled=True)


def spread(rows, pairs):
    return pair_a2a(jnp.broadcast_to(rows[None], (pairs,) + rows.shape))


def full_rows(x):
    return jnp.transpose(x, (1, 0, 2)).reshape(x.shape[1], -1)


def expert_pass(acts, grad, w_in, w_out, pairs):
    rows, width = acts.shape
    share = width // pairs
    af = acts.astype(F32)
    inv = lax.rsqrt(jnp.mean(af * af, axis=1) + 1e-06)
    normed = (af * inv[:, None]).astype(BF)
    pre = dot(normed, w_in, 1, 0)
    value, slope = gelu_both(pre)
    hidden = value.astype(BF)
    back = (dot(grad, w_out, 1, 1) * slope).astype(BF)
    part = dot(back, w_in, 1, 1)
    inner = jnp.sum(part * af, axis=1)
    high = inner.astype(BF)
    low = (inner - high.astype(F32)).astype(BF)
    extra = jnp.stack([high, low], axis=1)
    parts = jnp.transpose(part.astype(BF).reshape(rows, pairs, share), (1, 0, 2))
    parts = jnp.concatenate([parts, jnp.broadcast_to(extra[None], (pairs, rows, 2))], axis=2)
    got = pair_a2a(parts)
    total = jnp.sum(got.astype(F32), axis=0)
    mine = total[:, :share]
    inner = total[:, share] + total[:, share + 1]
    own = lax.dynamic_slice_in_dim(af, lax.axis_index("pair") * share, share, 1)
    branch = (inv[:, None] * mine - (inv**3 * inner / width)[:, None] * own).astype(BF)
    return branch, normed, back, hidden


def body(acts, cotangent, gates, owners, slots, w_in, w_out):
    core = lax.axis_index("segment")
    experts = lax.axis_size("expert")
    pairs = lax.axis_size("pair")
    tok, share = acts.shape[2:]
    cap = max(2, (5 * tok + 4 * experts - 1) // (4 * experts))
    rows = experts * cap
    acts = lax.dynamic_index_in_dim(acts, core, 1, False)
    cot = lax.dynamic_index_in_dim(cotangent, core, 0, False)
    gates = lax.dynamic_index_in_dim(gates, core, 1, False)
    owners = lax.dynamic_index_in_dim(owners, core, 1, False)
    slots = lax.dynamic_index_in_dim(slots, core, 1, False)
    own_in, own_out = w_in[0, 0], w_out[0, 0]
    other_in = lax.ppermute(own_in, "segment", SWAP)
    other_out = lax.ppermute(own_out, "segment", SWAP)
    top = core == 1
    in1 = jnp.where(top, own_in, other_in)
    in0 = jnp.where(top, other_in, own_in)
    out1 = jnp.where(top, own_out, other_out)
    out0 = jnp.where(top, other_out, own_out)

    place1 = one_hot(owners[1], slots[1], rows, cap)
    place0 = one_hot(owners[0], slots[0], rows, cap)
    scaled1 = (gates[1][:, None] * cot.astype(F32)).astype(BF)
    packed1 = dot(place1, jnp.concatenate([acts[1], scaled1], axis=1), 1, 0).astype(BF)
    packed0 = dot(place0, acts[0], 1, 0).astype(BF)
    first = jnp.concatenate([packed1, packed0], axis=1)
    got = expert_a2a(first.reshape(experts, cap, 3 * share)).reshape(rows, 3 * share)
    got = spread(got, pairs)
    rows1 = full_rows(got[:, :, :share])
    grad1 = full_rows(got[:, :, share : 2 * share])
    rows0 = full_rows(got[:, :, 2 * share :])

    branch1, normed1, back1, hidden1 = expert_pass(rows1, grad1, in1, out1, pairs)
    home = expert_a2a(branch1.reshape(experts, cap, share)).reshape(rows, share)
    res1 = (cot.astype(F32) + dot(place1, home, 0, 0)).astype(BF)

    scaled0 = (gates[0][:, None] * res1.astype(F32)).astype(BF)
    packed = dot(place0, scaled0, 1, 0).astype(BF)
    got = expert_a2a(packed.reshape(experts, cap, share)).reshape(rows, share)
    grad0 = full_rows(spread(got, pairs))
    branch0, normed0, back0, hidden0 = expert_pass(rows0, grad0, in0, out0, pairs)
    home = expert_a2a(branch0.reshape(experts, cap, share)).reshape(rows, share)
    res0 = (res1.astype(F32) + dot(place0, home, 0, 0)).astype(BF)

    first1, second1 = dot(normed1, back1, 0, 0), dot(hidden1, grad1, 0, 0)
    first0, second0 = dot(normed0, back0, 0, 0), dot(hidden0, grad0, 0, 0)
    keep_first, give_first = jnp.where(top, first1, first0), jnp.where(top, first0, first1)
    keep_second, give_second = jnp.where(top, second1, second0), jnp.where(top, second0, second1)
    got_first = lax.ppermute(give_first.astype(BF), "segment", SWAP)
    got_second = lax.ppermute(give_second.astype(BF), "segment", SWAP)
    grad_in = (keep_first + got_first.astype(F32)).astype(BF)
    grad_out = (keep_second + got_second.astype(F32)).astype(BF)

    keep, give = jnp.where(top, res1, res0), jnp.where(top, res0, res1)
    came = lax.ppermute(give, "segment", SWAP)
    grads = jnp.stack([jnp.where(top, came, keep), jnp.where(top, keep, came)])
    return grads[None], grad_in[None, None], grad_out[None, None]


def solution(mesh):
    placed = (
        P(None, None, "expert", "pair"),
        P(None, "expert", "pair"),
        P(None, None, "expert"),
        P(None, None, "expert"),
        P(None, None, "expert"),
        P("segment", "expert", None, "pair"),
        P("segment", "expert", "pair", None),
    )
    return jax.shard_map(
        body,
        mesh=mesh,
        in_specs=placed,
        out_specs=(
            P("segment", None, "expert", "pair"),
            P("segment", "expert", None, "pair"),
            P("segment", "expert", "pair", None),
        ),
        check_vma=False,
    )
```

```python
import functools

import jax
import jax.numpy as jnp
from jax import lax
from jax.experimental import pallas as pl
from jax.experimental.pallas import tpu as pltpu
from jax.sharding import Mesh, PartitionSpec as P

BF = jnp.bfloat16
F32 = jnp.float32
I32 = jnp.int32
SWAP = [(0, 1), (1, 0)]

NY, NZ, NX = 4, 16, 4
CAP = 4
TOK = 192
SHARE = 192
WIDTH = SHARE * NX
HID = 768
LOW = 128
ZROWS = NY * CAP + NY * CAP // 2
YROWS = NZ * CAP + NZ * CAP // 2
ALL = NZ * ZROWS


def dot(a, b, ca=1, cb=0):
    return lax.dot_general(a, b, (((ca,), (cb,)), ((), ())), preferred_element_type=F32)


def hot(cond):
    return jnp.where(cond, 1.0, 0.0).astype(BF)


def iota(shape, dim):
    return lax.broadcasted_iota(I32, shape, dim)


def column(row):
    n = row.shape[1]
    eye = iota((n, n), 0) == iota((n, n), 1)
    return jnp.sum(jnp.where(eye, row.astype(F32), 0.0), axis=1, keepdims=True)


def targets(owner, slot):
    base = (owner & (NZ - 1)) * ZROWS
    y = owner >> 4
    return base + y * CAP + slot, base + NY * CAP + y * 2 + (slot >> 1), slot & 1


def pack(values, owner, slot):
    low_at, high_at, odd = targets(owner, slot)
    at = iota((ALL, TOK), 0)
    low = hot(at == low_at)
    even_hot = hot((at == high_at) & (odd == 0))
    odd_hot = hot((at == high_at) & (odd == 1))
    out = []
    for v in values:
        high = v[:, LOW:]
        none = jnp.zeros_like(high)
        out.append(
            dot(low, v[:, :LOW])
            + dot(even_hot, jnp.concatenate([high, none], axis=1))
            + dot(odd_hot, jnp.concatenate([none, high], axis=1))
        )
    return out


def unpack(rows, owner, slot):
    low_at, high_at, odd = (column(t).astype(I32) for t in targets(owner, slot))
    at = iota((TOK, ALL), 1)
    low = dot(hot(at == low_at), rows)
    even_rows = dot(hot((at == high_at) & (odd == 0)), rows)
    odd_rows = dot(hot((at == high_at) & (odd == 1)), rows)
    high = even_rows[:, : SHARE - LOW] + odd_rows[:, SHARE - LOW :]
    return jnp.concatenate([low, high], axis=1)


def row_of(ref, layer, core):
    return jnp.where(core == 0, ref[layer, 0:1, :], ref[layer, 1:2, :])


def start_kernel(core_ref, acts, cot, gates, owners, slots, out, tok, gate_v, owner_v, slot_v, sems):
    core = core_ref[0]
    copies = [
        pltpu.make_async_copy(src, dst, sems.at[k])
        for k, (src, dst) in enumerate(
            [
                (owners, owner_v),
                (slots, slot_v),
                (gates, gate_v),
                (cot.at[core], tok.at[0]),
                (acts.at[1, core], tok.at[1]),
                (acts.at[0, core], tok.at[2]),
            ]
        )
    ]
    for copy in copies:
        copy.start()
    for copy in copies:
        copy.wait()
    gate = column(row_of(gate_v, 1, core))
    scaled = (gate * tok[0].astype(F32)).astype(BF)
    first = pack([tok[1], scaled], row_of(owner_v, 1, core), row_of(slot_v, 1, core))
    second = pack([tok[2]], row_of(owner_v, 0, core), row_of(slot_v, 0, core))
    parts = [p.reshape(NZ, ZROWS, LOW) for p in first + second]
    out[...] = jnp.concatenate(parts, axis=1).reshape(3 * ALL, LOW).astype(BF)


def spread_kernel(count, rows, out):
    shape = (NY, YROWS, ALL)
    y, k, at = iota(shape, 0), iota(shape, 1), iota(shape, 2)
    z = (k & 31) >> 1
    half = k & 1
    low = z * ZROWS + y * CAP + half * 2 + (k >> 5)
    high = z * ZROWS + NY * CAP + y * 2 + half
    move = hot((at == jnp.where(k < NZ * CAP, low, high)).reshape(ALL, ALL))
    value = rows[...].astype(F32).reshape(NZ, count * ZROWS, LOW)
    for a in range(count):
        part = value[:, a * ZROWS : (a + 1) * ZROWS].reshape(ALL, LOW).astype(BF)
        moved = dot(move, part).astype(BF)
        for j in range(NY):
            for i in range(NX):
                out[j * NX + i, a * YROWS : (a + 1) * YROWS, :] = moved[j * YROWS : (j + 1) * YROWS]


def gather_kernel(parts, out):
    shape = (NZ, ZROWS, ALL)
    z, k, at = iota(shape, 0), iota(shape, 1), iota(shape, 2)
    low = (k >> 2) * YROWS + (k & 1) * 32 + z * 2 + ((k & 3) >> 1)
    k2 = k - NY * CAP
    high = (k2 >> 1) * YROWS + NZ * CAP + z * 2 + (k2 & 1)
    move = hot((at == jnp.where(k < NY * CAP, low, high)).reshape(ALL, ALL))
    sums = []
    for j in range(NY):
        total = parts[j * NX].astype(F32)
        for i in range(1, NX):
            total = total + parts[j * NX + i].astype(F32)
        sums.append(total)
    out[...] = dot(move, jnp.concatenate(sums, axis=0).astype(BF)).astype(BF)


def assemble(ref, first):
    rows = []
    for j in range(NY):
        cols = []
        for i in range(NX):
            low = ref[j * NX + i, first : first + 64, :]
            high = ref[j * NX + i, first + 64 : first + YROWS, :]
            cols.append(low)
            cols.append(jnp.concatenate([high[:, :64], high[:, 64:]], axis=0))
        rows.append(jnp.concatenate(cols, axis=1))
    return jnp.concatenate(rows, axis=0)


def fetch(core, layer, own, other, into, sem):
    @pl.when(core == layer)
    def _():
        pltpu.make_async_copy(own, into, sem).start()

    @pl.when(core != layer)
    def _():
        pltpu.make_async_copy(other, into, sem).start()

    return pltpu.make_async_copy(own, into, sem)


def expert_kernel(
    layer, acts_at, grad_at, core_ref, acts_ref, grad_ref, own_in, other_in, own_out, other_out,
    out, kept_out, in_ref, out_ref, kept, sems,
):
    core = core_ref[0]
    first = fetch(core, layer, own_in, other_in, in_ref, sems.at[0])
    second = fetch(core, layer, own_out, other_out, out_ref, sems.at[1])
    saves = [pltpu.make_async_copy(kept.at[k], kept_out.at[k], sems.at[2 + k]) for k in range(4)]

    def save(k, value):
        kept[k] = value
        saves[k].start()

    x = assemble(acts_ref, acts_at).astype(F32)
    grad = assemble(grad_ref, grad_at)
    save(3, grad)
    inv = lax.rsqrt(jnp.mean(x * x, axis=1, keepdims=True) + 1e-06)
    normed = (x * inv).astype(BF)
    save(0, normed)
    first.wait()
    u = dot(normed, in_ref[...])
    square = u * u
    s = jnp.tanh(0.7978845608 * (u + 0.044715 * square * u))
    save(2, (0.5 * u * (1.0 + s)).astype(BF))
    slope = 0.5 * (1.0 + s) + 0.5 * u * (1.0 - s * s) * 0.7978845608 * (1.0 + 0.134145 * square)
    second.wait()
    back = (dot(grad, out_ref[...], 1, 1) * slope).astype(BF)
    save(1, back)
    part = dot(back, in_ref[...], 1, 1)
    inner = jnp.sum(part * x, axis=1, keepdims=True)
    branch = (inv * part - (inv * inv * inv * inner * (1.0 / WIDTH)) * x).astype(BF)
    for j in range(NY):
        for i in range(NX):
            at = i * SHARE
            block = branch[j * 64 : (j + 1) * 64]
            out[j * NX + i, 0:64, :] = block[:, at : at + LOW]
            out[j * NX + i, 64:YROWS, :] = jnp.concatenate(
                [block[:32, at + LOW : at + SHARE], block[32:, at + LOW : at + SHARE]], axis=1
            )
    for copy in saves:
        copy.wait()


def weight_kernel(core_ref, kept1, came1, kept0, came0, first, second, mark, rows, sums, sems):
    core = core_ref[0]
    half = NY * NZ * CAP
    for index, sources in enumerate([(kept0, came0), (kept1, came1)]):

        @pl.when(core == index)
        def _():
            for k in range(4):
                for n, src in enumerate(sources):
                    pltpu.make_async_copy(src.at[k], rows.at[k, n * half : (n + 1) * half], sems.at[2 * k + n]).start()

    def product(k, at, dst):
        for i in (k, k + 1):
            for n in range(2):
                pltpu.make_async_copy(kept1.at[i], rows.at[i, n * half : (n + 1) * half], sems.at[2 * i + n]).wait()
        sums[at] = dot(rows[k], rows[k + 1], 0, 0).astype(BF)
        copy = pltpu.make_async_copy(sums.at[at], dst, sems.at[8 + at])
        copy.start()
        return copy

    stores = [product(0, 0, first), product(2, 1, second)]
    mark[...] = jnp.zeros_like(mark)
    for copy in stores:
        copy.wait()


def middle_kernel(core_ref, rows, cot, gates, owners, slots, result, out):
    core = core_ref[0]
    branch = unpack(rows[...], row_of(owners, 1, core), row_of(slots, 1, core))
    res = (cot[core].astype(F32) + branch).astype(BF)
    result[...] = res
    gate = column(row_of(gates, 0, core))
    scaled = (gate * res.astype(F32)).astype(BF)
    (packed,) = pack([scaled], row_of(owners, 0, core), row_of(slots, 0, core))
    out[...] = packed.astype(BF)


def end_kernel(core_ref, rows, above, owners, slots, mark, keep, give):
    core = core_ref[0]
    branch = unpack(rows[...], row_of(owners, 0, core), row_of(slots, 0, core))
    res = (above[...].astype(F32) + branch).astype(BF)
    keep[...] = jnp.where(core == 0, res, above[...])
    give[...] = jnp.where(core == 0, above[...], res)


VM = pl.BlockSpec(memory_space=pltpu.VMEM)
SM = pl.BlockSpec(memory_space=pltpu.SMEM)
HB = pl.BlockSpec(memory_space=pltpu.HBM)


def call(kernel, ins, outs, name, scratch=(), mib=16, cost=None, places=None):
    return pl.pallas_call(
        kernel,
        in_specs=list(ins),
        out_specs=places or [VM] * len(outs),
        out_shape=[jax.ShapeDtypeStruct(o, BF) for o in outs],
        scratch_shapes=list(scratch),
        compiler_params=pltpu.CompilerParams(vmem_limit_bytes=mib << 20),
        cost_estimate=cost and pl.CostEstimate(flops=cost[0], bytes_accessed=cost[1], transcendentals=0),
        name=name,
    )


def a2a(x, axis):
    return lax.all_to_all(x, axis, split_axis=0, concat_axis=0, tiled=True)


def over_z(x):
    return a2a(x.reshape(NZ, -1, LOW), "z").reshape(-1, LOW)


def over_yx(x):
    return a2a(x, ("y", "pair"))


def expert(layer, acts_at, grad_at, core, acts, grad, weights):
    rows = (NY * NZ * CAP, WIDTH)
    return call(
        functools.partial(expert_kernel, layer, acts_at, grad_at),
        [SM, VM, VM] + [HB] * 4,
        [(NY * NX, YROWS, LOW), (4,) + rows],
        "expert",
        [
            pltpu.VMEM((WIDTH, HID), BF),
            pltpu.VMEM((HID, WIDTH), BF),
            pltpu.VMEM((4,) + rows, BF),
            pltpu.SemaphoreType.DMA((6,)),
        ],
        places=[VM, HB],
    )(core, acts, grad, *weights)


def body(acts, cotangent, gates, owners, slots, w_in, w_out):
    index = lax.axis_index("segment")
    top = index == 1
    core = index.astype(I32).reshape(1)
    own_in, own_out = w_in[0, 0], w_out[0, 0]
    other_in = lax.ppermute(own_in, "segment", SWAP)
    other_out = lax.ppermute(own_out, "segment", SWAP)
    weights = (own_in, other_in, own_out, other_out)

    table = (2, 2, TOK)
    (packed,) = call(
        start_kernel, [SM] + [HB] * 5, [(3 * ALL, LOW)], "start",
        [pltpu.VMEM((3, TOK, SHARE), BF), pltpu.VMEM(table, F32), pltpu.VMEM(table, I32),
         pltpu.VMEM(table, I32), pltpu.SemaphoreType.DMA((6,))], mib=60,
    )(core, acts, cotangent, gates, owners, slots)
    (sent,) = call(functools.partial(spread_kernel, 3), [VM], [(NY * NX, 3 * YROWS, LOW)], "spread3")(
        over_z(packed)
    )
    saved = over_yx(sent)
    parts, kept1 = expert(1, 0, YROWS, core, saved, saved, weights)
    came1 = lax.ppermute(kept1, "segment", [(0, 1)])
    (rows,) = call(gather_kernel, [VM], [(ALL, LOW)], "gather")(over_yx(parts))
    res1, packed = call(middle_kernel, [SM] + [VM] * 5, [(TOK, SHARE), (ALL, LOW)], "middle")(
        core, over_z(rows), cotangent, gates, owners, slots
    )
    (sent,) = call(functools.partial(spread_kernel, 1), [VM], [(NY * NX, YROWS, LOW)], "spread1")(
        over_z(packed)
    )
    parts, kept0 = expert(0, 2 * YROWS, 0, core, saved, over_yx(sent), weights)
    (rows,) = call(gather_kernel, [VM], [(ALL, LOW)], "gather")(over_yx(parts))

    came0 = lax.ppermute(kept0, "segment", [(1, 0)])
    grad_in, grad_out, mark = call(
        weight_kernel, [SM] + [HB] * 4, [(WIDTH, HID), (HID, WIDTH), (16, 128)], "weight",
        [pltpu.VMEM((4, 2 * NY * NZ * CAP, WIDTH), BF), pltpu.VMEM((2, WIDTH, HID), BF), pltpu.SemaphoreType.DMA((10,))],
        mib=24, cost=(2 * 10**9, 6 * 10**6), places=[HB, HB, VM],
    )(core, kept1, came1, kept0, came0)
    mine, other = call(end_kernel, [SM] + [VM] * 5, [(TOK, SHARE)] * 2, "end")(
        core, over_z(rows), res1, owners, slots, mark
    )
    got = lax.ppermute(other, "segment", SWAP)
    grads = jnp.stack([jnp.where(top, got, mine), jnp.where(top, mine, got)])
    return grads[None], grad_in[None, None], grad_out[None, None]


def solution(mesh):
    fine = Mesh(mesh.devices.reshape(2, NY, NZ, NX), ("segment", "y", "z", "pair"))
    e = ("y", "z")
    placed = (
        P(None, None, e, "pair"),
        P(None, e, "pair"),
        P(None, None, e),
        P(None, None, e),
        P(None, None, e),
        P("segment", e, None, "pair"),
        P("segment", e, "pair", None),
    )
    return jax.shard_map(
        body,
        mesh=fine,
        in_specs=placed,
        out_specs=(
            P("segment", None, e, "pair"),
            P("segment", e, None, "pair"),
            P("segment", e, "pair", None),
        ),
        check_vma=False,
    )
```

```python
import functools

import jax
import jax.numpy as jnp
from jax import lax
from jax.experimental import pallas as pl
from jax.experimental.pallas import tpu as pltpu
from jax.sharding import Mesh, PartitionSpec as P

BF = jnp.bfloat16
F32 = jnp.float32
I32 = jnp.int32
SWAP = [(0, 1), (1, 0)]

NY, NZ, NX = 4, 16, 4
CAP = 4
TOK = 192
SHARE = 192
WIDTH = SHARE * NX
HID = 768
LOW = 128
ZROWS = NY * CAP + NY * CAP // 2
YROWS = NZ * CAP + NZ * CAP // 2
ALL = NZ * ZROWS


def dot(a, b, ca=1, cb=0):
    return lax.dot_general(a, b, (((ca,), (cb,)), ((), ())), preferred_element_type=F32)


def hot(cond):
    return jnp.where(cond, 1.0, 0.0).astype(BF)


def iota(shape, dim):
    return lax.broadcasted_iota(I32, shape, dim)


def column(row):
    n = row.shape[1]
    eye = iota((n, n), 0) == iota((n, n), 1)
    return jnp.sum(jnp.where(eye, row.astype(F32), 0.0), axis=1, keepdims=True)


def targets(owner, slot):
    base = (owner & (NZ - 1)) * ZROWS
    y = owner >> 4
    return base + y * CAP + slot, base + NY * CAP + y * 2 + (slot >> 1), slot & 1


def pack(values, owner, slot):
    low_at, high_at, odd = targets(owner, slot)
    at = iota((ALL, TOK), 0)
    low = hot(at == low_at)
    even_hot = hot((at == high_at) & (odd == 0))
    odd_hot = hot((at == high_at) & (odd == 1))
    out = []
    for v in values:
        high = v[:, LOW:]
        none = jnp.zeros_like(high)
        out.append(
            dot(low, v[:, :LOW])
            + dot(even_hot, jnp.concatenate([high, none], axis=1))
            + dot(odd_hot, jnp.concatenate([none, high], axis=1))
        )
    return out


def unpack(rows, owner, slot):
    low_at, high_at, odd = (column(t).astype(I32) for t in targets(owner, slot))
    at = iota((TOK, ALL), 1)
    low = dot(hot(at == low_at), rows)
    even_rows = dot(hot((at == high_at) & (odd == 0)), rows)
    odd_rows = dot(hot((at == high_at) & (odd == 1)), rows)
    high = even_rows[:, : SHARE - LOW] + odd_rows[:, SHARE - LOW :]
    return jnp.concatenate([low, high], axis=1)


def row_of(ref, layer, core):
    return jnp.where(core == 0, ref[layer, 0:1, :], ref[layer, 1:2, :])


def start_kernel(core_ref, acts, cot, gates, owners, slots, out, tok, gate_v, owner_v, slot_v, sems):
    core = core_ref[0]
    copies = [
        pltpu.make_async_copy(src, dst, sems.at[k])
        for k, (src, dst) in enumerate(
            [
                (owners, owner_v),
                (slots, slot_v),
                (gates, gate_v),
                (cot.at[core], tok.at[0]),
                (acts.at[1, core], tok.at[1]),
                (acts.at[0, core], tok.at[2]),
            ]
        )
    ]
    for copy in copies:
        copy.start()
    for copy in copies:
        copy.wait()
    gate = column(row_of(gate_v, 1, core))
    scaled = (gate * tok[0].astype(F32)).astype(BF)
    first = pack([tok[1], scaled], row_of(owner_v, 1, core), row_of(slot_v, 1, core))
    second = pack([tok[2]], row_of(owner_v, 0, core), row_of(slot_v, 0, core))
    parts = [p.reshape(NZ, ZROWS, LOW) for p in first + second]
    out[...] = jnp.concatenate(parts, axis=1).reshape(3 * ALL, LOW).astype(BF)


def spread_kernel(count, rows, out):
    shape = (NY, YROWS, ALL)
    y, k, at = iota(shape, 0), iota(shape, 1), iota(shape, 2)
    z = (k & 31) >> 1
    half = k & 1
    low = z * ZROWS + y * CAP + half * 2 + (k >> 5)
    high = z * ZROWS + NY * CAP + y * 2 + half
    move = hot((at == jnp.where(k < NZ * CAP, low, high)).reshape(ALL, ALL))
    value = rows[...].astype(F32).reshape(NZ, count * ZROWS, LOW)
    for a in range(count):
        part = value[:, a * ZROWS : (a + 1) * ZROWS].reshape(ALL, LOW).astype(BF)
        moved = dot(move, part).astype(BF)
        for j in range(NY):
            for i in range(NX):
                out[j * NX + i, a * YROWS : (a + 1) * YROWS, :] = moved[j * YROWS : (j + 1) * YROWS]


def gather_kernel(parts, out):
    shape = (NZ, ZROWS, ALL)
    z, k, at = iota(shape, 0), iota(shape, 1), iota(shape, 2)
    low = (k >> 2) * YROWS + (k & 1) * 32 + z * 2 + ((k & 3) >> 1)
    k2 = k - NY * CAP
    high = (k2 >> 1) * YROWS + NZ * CAP + z * 2 + (k2 & 1)
    move = hot((at == jnp.where(k < NY * CAP, low, high)).reshape(ALL, ALL))
    sums = []
    for j in range(NY):
        total = parts[j * NX].astype(F32)
        for i in range(1, NX):
            total = total + parts[j * NX + i].astype(F32)
        sums.append(total)
    out[...] = dot(move, jnp.concatenate(sums, axis=0).astype(BF)).astype(BF)


def assemble(ref, first):
    rows = []
    for j in range(NY):
        cols = []
        for i in range(NX):
            low = ref[j * NX + i, first : first + 64, :]
            high = ref[j * NX + i, first + 64 : first + YROWS, :]
            cols.append(low)
            cols.append(jnp.concatenate([high[:, :64], high[:, 64:]], axis=0))
        rows.append(jnp.concatenate(cols, axis=1))
    return jnp.concatenate(rows, axis=0)


def expert_step(x, grad, w_in, w_out, out, save):
    save(3, grad)
    inv = lax.rsqrt(jnp.mean(x * x, axis=1, keepdims=True) + 1e-06)
    normed = (x * inv).astype(BF)
    save(0, normed)
    u = dot(normed, w_in[...])
    square = u * u
    s = jnp.tanh(0.7978845608 * (u + 0.044715 * square * u))
    save(2, (0.5 * u * (1.0 + s)).astype(BF))
    slope = 0.5 * (1.0 + s) + 0.5 * u * (1.0 - s * s) * 0.7978845608 * (1.0 + 0.134145 * square)
    back = (dot(grad, w_out[...], 1, 1) * slope).astype(BF)
    save(1, back)
    part = dot(back, w_in[...], 1, 1)
    inner = jnp.sum(part * x, axis=1, keepdims=True)
    branch = (inv * part - (inv * inv * inv * inner * (1.0 / WIDTH)) * x).astype(BF)
    for j in range(NY):
        for i in range(NX):
            at = i * SHARE
            block = branch[j * 64 : (j + 1) * 64]
            out[j * NX + i, 0:64, :] = block[:, at : at + LOW]
            out[j * NX + i, 64:YROWS, :] = jnp.concatenate(
                [block[:32, at + LOW : at + SHARE], block[32:, at + LOW : at + SHARE]], axis=1
            )


def upper_kernel(core_ref, saved, own_in, other_in, own_out, other_out, out, *kept):
    def run(w_in, w_out):
        def save(k, value):
            kept[k][...] = value

        expert_step(assemble(saved, 0).astype(F32), assemble(saved, YROWS), w_in, w_out, out, save)

    @pl.when(core_ref[0] == 1)
    def _():
        run(own_in, own_out)

    @pl.when(core_ref[0] != 1)
    def _():
        run(other_in, other_out)


def lower_kernel(
    core_ref, saved, came, n1, b1, h1, g1, own_in, other_in, own_out, other_out,
    out, k0, k1, k2, k3, give, kept, sems,
):
    keep, above = (k0, k1, k2, k3), (n1, b1, h1, g1)

    def run(w_in, w_out, save):
        expert_step(assemble(saved, 2 * YROWS).astype(F32), assemble(came, 0), w_in, w_out, out, save)

    @pl.when(core_ref[0] == 0)
    def _():
        copies = [pltpu.make_async_copy(above[k], give.at[k], sems.at[k]) for k in range(4)]
        for copy in copies:
            copy.start()

        def save(k, value):
            keep[k][...] = value

        run(own_in, own_out, save)
        for copy in copies:
            copy.wait()

    @pl.when(core_ref[0] != 0)
    def _():
        copies = [pltpu.make_async_copy(kept.at[k], give.at[k], sems.at[k]) for k in range(4)]

        def save(k, value):
            kept[k] = value
            copies[k].start()
            keep[k][...] = above[k][...]

        run(other_in, other_out, save)
        for copy in copies:
            copy.wait()


def weight_kernel(k0, k1, k2, k3, came, first, second, mark, rows, sums, sems):
    half = NY * NZ * CAP
    loads = [
        [pltpu.make_async_copy(src, rows.at[k, n * half : (n + 1) * half], sems.at[2 * k + n])
         for n, src in enumerate([(k0, k1, k2, k3)[k], came.at[k]])]
        for k in range(4)
    ]
    for pair in loads:
        for copy in pair:
            copy.start()

    def product(k, at, dst):
        for copy in loads[k] + loads[k + 1]:
            copy.wait()
        sums[at] = dot(rows[k], rows[k + 1], 0, 0).astype(BF)
        copy = pltpu.make_async_copy(sums.at[at], dst, sems.at[8 + at])
        copy.start()
        return copy

    stores = [product(0, 0, first), product(2, 1, second)]
    mark[...] = jnp.zeros_like(mark)
    for copy in stores:
        copy.wait()


def middle_kernel(core_ref, rows, cot, gates, owners, slots, result, out):
    core = core_ref[0]
    branch = unpack(rows[...], row_of(owners, 1, core), row_of(slots, 1, core))
    res = (cot[core].astype(F32) + branch).astype(BF)
    result[...] = res
    gate = column(row_of(gates, 0, core))
    scaled = (gate * res.astype(F32)).astype(BF)
    (packed,) = pack([scaled], row_of(owners, 0, core), row_of(slots, 0, core))
    out[...] = packed.astype(BF)


def end_kernel(core_ref, rows, above, owners, slots, mark, keep, give):
    core = core_ref[0]
    branch = unpack(rows[...], row_of(owners, 0, core), row_of(slots, 0, core))
    res = (above[...].astype(F32) + branch).astype(BF)
    keep[...] = jnp.where(core == 0, res, above[...])
    give[...] = jnp.where(core == 0, above[...], res)


VM = pl.BlockSpec(memory_space=pltpu.VMEM)
SM = pl.BlockSpec(memory_space=pltpu.SMEM)
HB = pl.BlockSpec(memory_space=pltpu.HBM)


def call(kernel, ins, outs, name, scratch=(), mib=16, cost=None, places=None):
    return pl.pallas_call(
        kernel,
        in_specs=list(ins),
        out_specs=places or [VM] * len(outs),
        out_shape=[jax.ShapeDtypeStruct(o, BF) for o in outs],
        scratch_shapes=list(scratch),
        compiler_params=pltpu.CompilerParams(vmem_limit_bytes=mib << 20),
        cost_estimate=cost and pl.CostEstimate(flops=cost[0], bytes_accessed=cost[1], transcendentals=0),
        name=name,
    )


def a2a(x, axis):
    return lax.all_to_all(x, axis, split_axis=0, concat_axis=0, tiled=True)


def over_z(x):
    return a2a(x.reshape(NZ, -1, LOW), "z").reshape(-1, LOW)


def over_yx(x):
    return a2a(x, ("y", "pair"))


def body(acts, cotangent, gates, owners, slots, w_in, w_out):
    index = lax.axis_index("segment")
    top = index == 1
    core = index.astype(I32).reshape(1)
    own_in, own_out = w_in[0, 0], w_out[0, 0]
    other_in = lax.ppermute(own_in, "segment", SWAP)
    other_out = lax.ppermute(own_out, "segment", SWAP)
    weights = (own_in, other_in, own_out, other_out)

    table = (2, 2, TOK)
    (packed,) = call(
        start_kernel, [SM] + [HB] * 5, [(3 * ALL, LOW)], "start",
        [pltpu.VMEM((3, TOK, SHARE), BF), pltpu.VMEM(table, F32), pltpu.VMEM(table, I32),
         pltpu.VMEM(table, I32), pltpu.SemaphoreType.DMA((6,))], mib=60,
    )(core, acts, cotangent, gates, owners, slots)
    (sent,) = call(functools.partial(spread_kernel, 3), [VM], [(NY * NX, 3 * YROWS, LOW)], "spread3", mib=16)(
        over_z(packed)
    )
    saved = over_yx(sent)
    blocks, wide = (NY * NX, YROWS, LOW), (NY * NZ * CAP, WIDTH)
    parts, *kept1 = call(upper_kernel, [SM] + [VM] * 5, [blocks] + [wide] * 4, "upper")(core, saved, *weights)
    (rows,) = call(gather_kernel, [VM], [(ALL, LOW)], "gather")(over_yx(parts))
    res1, packed = call(middle_kernel, [SM] + [VM] * 5, [(TOK, SHARE), (ALL, LOW)], "middle")(
        core, over_z(rows), cotangent, gates, owners, slots
    )
    (sent,) = call(functools.partial(spread_kernel, 1), [VM], [(NY * NX, YROWS, LOW)], "spread1")(
        over_z(packed)
    )
    parts, *keep, give = call(
        lower_kernel, [SM] + [VM] * 10, [blocks] + [wide] * 4 + [(4,) + wide], "lower",
        [pltpu.VMEM((4,) + wide, BF), pltpu.SemaphoreType.DMA((4,))], places=[VM] * 5 + [HB],
    )(core, saved, over_yx(sent), *kept1, *weights)
    came = lax.ppermute(give, "segment", SWAP)
    (rows,) = call(gather_kernel, [VM], [(ALL, LOW)], "gather")(over_yx(parts))

    grad_in, grad_out, mark = call(
        weight_kernel, [HB] * 5, [(WIDTH, HID), (HID, WIDTH), (16, 128)], "weight",
        [pltpu.VMEM((4, 2 * NY * NZ * CAP, WIDTH), BF), pltpu.VMEM((2, WIDTH, HID), BF), pltpu.SemaphoreType.DMA((10,))],
        mib=16, cost=(2 * 10**9, 6 * 10**6), places=[HB, HB, VM],
    )(*keep, came)
    mine, other = call(end_kernel, [SM] + [VM] * 5, [(TOK, SHARE)] * 2, "end")(
        core, over_z(rows), res1, owners, slots, mark
    )
    got = lax.ppermute(other, "segment", SWAP)
    grads = jnp.stack([jnp.where(top, got, mine), jnp.where(top, mine, got)])
    return grads[None], grad_in[None, None], grad_out[None, None]


def solution(mesh):
    fine = Mesh(mesh.devices.reshape(2, NY, NZ, NX), ("segment", "y", "z", "pair"))
    e = ("y", "z")
    placed = (
        P(None, None, e, "pair"),
        P(None, e, "pair"),
        P(None, None, e),
        P(None, None, e),
        P(None, None, e),
        P("segment", e, None, "pair"),
        P("segment", e, "pair", None),
    )
    return jax.shard_map(
        body,
        mesh=fine,
        in_specs=placed,
        out_specs=(
            P("segment", None, e, "pair"),
            P("segment", e, None, "pair"),
            P("segment", e, "pair", None),
        ),
        check_vma=False,
    )
```

```python
import functools

import jax
import jax.numpy as jnp
from jax import lax
from jax.experimental import pallas as pl
from jax.experimental.pallas import tpu as pltpu
from jax.sharding import Mesh, PartitionSpec as P

BF = jnp.bfloat16
F32 = jnp.float32
I32 = jnp.int32
SWAP = [(0, 1), (1, 0)]

NY, NZ, NX = 4, 16, 4
CAP = 4
TOK = 192
SHARE = 192
WIDTH = SHARE * NX
FIRST = NZ // 2
HID = 768
LOW = 128
ZROWS = NY * CAP + NY * CAP // 2
YROWS = NZ * CAP + NZ * CAP // 2
ALL = NZ * ZROWS


def dot(a, b, ca=1, cb=0):
    return lax.dot_general(a, b, (((ca,), (cb,)), ((), ())), preferred_element_type=F32)


def hot(cond):
    return jnp.where(cond, 1.0, 0.0).astype(BF)


def iota(shape, dim):
    return lax.broadcasted_iota(I32, shape, dim)


def column(row):
    n = row.shape[1]
    eye = iota((n, n), 0) == iota((n, n), 1)
    return jnp.sum(jnp.where(eye, row.astype(F32), 0.0), axis=1, keepdims=True)


def targets(owner, slot):
    base = ((owner + FIRST) & (NZ - 1)) * ZROWS
    y = owner >> 4
    return base + y * CAP + slot, base + NY * CAP + y * 2 + (slot >> 1), slot & 1


def pack(values, owner, slot):
    low_at, high_at, odd = targets(owner, slot)
    at = iota((ALL, TOK), 0)
    low = hot(at == low_at)
    even_hot = hot((at == high_at) & (odd == 0))
    odd_hot = hot((at == high_at) & (odd == 1))
    out = []
    for v in values:
        high = v[:, LOW:]
        none = jnp.zeros_like(high)
        out.append(
            dot(low, v[:, :LOW])
            + dot(even_hot, jnp.concatenate([high, none], axis=1))
            + dot(odd_hot, jnp.concatenate([none, high], axis=1))
        )
    return out


def unpack(rows, owner, slot):
    low_at, high_at, odd = (column(t).astype(I32) for t in targets(owner, slot))
    at = iota((TOK, ALL), 1)
    low = dot(hot(at == low_at), rows)
    even_rows = dot(hot((at == high_at) & (odd == 0)), rows)
    odd_rows = dot(hot((at == high_at) & (odd == 1)), rows)
    high = even_rows[:, : SHARE - LOW] + odd_rows[:, SHARE - LOW :]
    return jnp.concatenate([low, high], axis=1)


def row_of(ref, layer, core):
    return jnp.where(core == 0, ref[layer, 0:1, :], ref[layer, 1:2, :])


def start_kernel(core_ref, acts, cot, gates, owners, slots, out, tok, gate_v, owner_v, slot_v, sems):
    core = core_ref[0]
    copies = [
        pltpu.make_async_copy(src, dst, sems.at[k])
        for k, (src, dst) in enumerate(
            [
                (owners, owner_v),
                (slots, slot_v),
                (gates, gate_v),
                (cot.at[core], tok.at[0]),
                (acts.at[1, core], tok.at[1]),
                (acts.at[0, core], tok.at[2]),
            ]
        )
    ]
    for copy in copies:
        copy.start()
    for copy in copies:
        copy.wait()
    gate = column(row_of(gate_v, 1, core))
    scaled = (gate * tok[0].astype(F32)).astype(BF)
    first = pack([tok[1], scaled], row_of(owner_v, 1, core), row_of(slot_v, 1, core))
    second = pack([tok[2]], row_of(owner_v, 0, core), row_of(slot_v, 0, core))
    parts = [p.reshape(NZ, ZROWS, LOW) for p in first + second]
    out[...] = jnp.concatenate(parts, axis=1).reshape(3 * ALL, LOW).astype(BF)


def spread_kernel(count, rows, out):
    shape = (NY, YROWS, ALL)
    y, k, at = iota(shape, 0), iota(shape, 1), iota(shape, 2)
    z = (k & 31) >> 1
    half = k & 1
    low = z * ZROWS + y * CAP + half * 2 + (k >> 5)
    high = z * ZROWS + NY * CAP + y * 2 + half
    move = hot((at == jnp.where(k < NZ * CAP, low, high)).reshape(ALL, ALL))
    value = rows[...].astype(F32).reshape(NZ, count * ZROWS, LOW)
    for a in range(count):
        part = value[:, a * ZROWS : (a + 1) * ZROWS].reshape(ALL, LOW).astype(BF)
        moved = dot(move, part).astype(BF)
        for j in range(NY):
            for i in range(NX):
                out[j * NX + i, a * YROWS : (a + 1) * YROWS, :] = moved[j * YROWS : (j + 1) * YROWS]


def gather_kernel(parts, out):
    shape = (NZ, ZROWS, ALL)
    z, k, at = iota(shape, 0), iota(shape, 1), iota(shape, 2)
    low = (k >> 2) * YROWS + (k & 1) * 32 + z * 2 + ((k & 3) >> 1)
    k2 = k - NY * CAP
    high = (k2 >> 1) * YROWS + NZ * CAP + z * 2 + (k2 & 1)
    move = hot((at == jnp.where(k < NY * CAP, low, high)).reshape(ALL, ALL))
    sums = []
    for j in range(NY):
        total = parts[j * NX].astype(F32)
        for i in range(1, NX):
            total = total + parts[j * NX + i].astype(F32)
        sums.append(total)
    out[...] = dot(move, jnp.concatenate(sums, axis=0).astype(BF)).astype(BF)


def assemble(ref, first):
    rows = []
    for j in range(NY):
        cols = []
        for i in range(NX):
            low = ref[j * NX + i, first : first + 64, :]
            high = ref[j * NX + i, first + 64 : first + YROWS, :]
            cols.append(low)
            cols.append(jnp.concatenate([high[:, :64], high[:, 64:]], axis=0))
        rows.append(jnp.concatenate(cols, axis=1))
    return jnp.concatenate(rows, axis=0)


def expert_step(x, grad, w_in, w_out, out, save):
    save(3, grad)
    inv = lax.rsqrt(jnp.mean(x * x, axis=1, keepdims=True) + 1e-06)
    normed = (x * inv).astype(BF)
    save(0, normed)
    u = dot(normed, w_in[...])
    square = u * u
    s = jnp.tanh(0.7978845608 * (u + 0.044715 * square * u))
    save(2, (0.5 * u * (1.0 + s)).astype(BF))
    slope = 0.5 * (1.0 + s) + 0.5 * u * (1.0 - s * s) * 0.7978845608 * (1.0 + 0.134145 * square)
    back = (dot(grad, w_out[...], 1, 1) * slope).astype(BF)
    save(1, back)
    part = dot(back, w_in[...], 1, 1)
    inner = jnp.sum(part * x, axis=1, keepdims=True)
    branch = (inv * part - (inv * inv * inv * inner * (1.0 / WIDTH)) * x).astype(BF)
    for j in range(NY):
        for i in range(NX):
            at = i * SHARE
            block = branch[j * 64 : (j + 1) * 64]
            out[j * NX + i, 0:64, :] = block[:, at : at + LOW]
            out[j * NX + i, 64:YROWS, :] = jnp.concatenate(
                [block[:32, at + LOW : at + SHARE], block[32:, at + LOW : at + SHARE]], axis=1
            )


def upper_kernel(core_ref, saved, own_in, other_in, own_out, other_out, out, *kept):
    def run(w_in, w_out):
        def save(k, value):
            kept[k][...] = value

        expert_step(assemble(saved, 0).astype(F32), assemble(saved, YROWS), w_in, w_out, out, save)

    @pl.when(core_ref[0] == 1)
    def _():
        run(own_in, own_out)

    @pl.when(core_ref[0] != 1)
    def _():
        run(other_in, other_out)


def lower_kernel(
    core_ref, saved, came, n1, b1, h1, g1, own_in, other_in, own_out, other_out,
    out, k0, k1, k2, k3, give, kept, sems,
):
    keep, above = (k0, k1, k2, k3), (n1, b1, h1, g1)

    def run(w_in, w_out, save):
        expert_step(assemble(saved, 2 * YROWS).astype(F32), assemble(came, 0), w_in, w_out, out, save)

    @pl.when(core_ref[0] == 0)
    def _():
        copies = [pltpu.make_async_copy(above[k], give.at[k], sems.at[k]) for k in range(4)]
        for copy in copies:
            copy.start()

        def save(k, value):
            keep[k][...] = value

        run(own_in, own_out, save)
        for copy in copies:
            copy.wait()

    @pl.when(core_ref[0] != 0)
    def _():
        copies = [pltpu.make_async_copy(kept.at[k], give.at[k], sems.at[k]) for k in range(4)]

        def save(k, value):
            kept[k] = value
            copies[k].start()
            keep[k][...] = above[k][...]

        run(other_in, other_out, save)
        for copy in copies:
            copy.wait()


def weight_kernel(k0, k1, k2, k3, came, first, second, mark, rows, sums, sems):
    half = NY * NZ * CAP
    loads = [
        [pltpu.make_async_copy(src, rows.at[k, n * half : (n + 1) * half], sems.at[2 * k + n])
         for n, src in enumerate([(k0, k1, k2, k3)[k], came.at[k]])]
        for k in range(4)
    ]
    for pair in loads:
        for copy in pair:
            copy.start()

    def product(k, at, dst):
        for copy in loads[k] + loads[k + 1]:
            copy.wait()
        sums[at] = dot(rows[k], rows[k + 1], 0, 0).astype(BF)
        copy = pltpu.make_async_copy(sums.at[at], dst, sems.at[8 + at])
        copy.start()
        return copy

    stores = [product(0, 0, first), product(2, 1, second)]
    mark[...] = jnp.zeros_like(mark)
    for copy in stores:
        copy.wait()


def middle_kernel(core_ref, rows, cot, gates, owners, slots, result, out):
    core = core_ref[0]
    branch = unpack(rows[...], row_of(owners, 1, core), row_of(slots, 1, core))
    res = (cot[core].astype(F32) + branch).astype(BF)
    result[...] = res
    gate = column(row_of(gates, 0, core))
    scaled = (gate * res.astype(F32)).astype(BF)
    (packed,) = pack([scaled], row_of(owners, 0, core), row_of(slots, 0, core))
    out[...] = packed.astype(BF)


def end_kernel(core_ref, rows, above, owners, slots, mark, keep, give):
    core = core_ref[0]
    branch = unpack(rows[...], row_of(owners, 0, core), row_of(slots, 0, core))
    res = (above[...].astype(F32) + branch).astype(BF)
    keep[...] = jnp.where(core == 0, res, above[...])
    give[...] = jnp.where(core == 0, above[...], res)


VM = pl.BlockSpec(memory_space=pltpu.VMEM)
SM = pl.BlockSpec(memory_space=pltpu.SMEM)
HB = pl.BlockSpec(memory_space=pltpu.HBM)


def call(kernel, ins, outs, name, scratch=(), mib=16, cost=None, places=None):
    return pl.pallas_call(
        kernel,
        in_specs=list(ins),
        out_specs=places or [VM] * len(outs),
        out_shape=[jax.ShapeDtypeStruct(o, BF) for o in outs],
        scratch_shapes=list(scratch),
        compiler_params=pltpu.CompilerParams(vmem_limit_bytes=mib << 20),
        cost_estimate=cost and pl.CostEstimate(flops=cost[0], bytes_accessed=cost[1], transcendentals=0),
        name=name,
    )


def over_z(x):
    ring = [[(FIRST + k) % NZ for k in range(NZ)]]
    x = x.reshape(NZ, -1, LOW)
    return lax.all_to_all(x, "z", 0, 0, axis_index_groups=ring, tiled=True).reshape(-1, LOW)


def over_yx(x):
    return lax.all_to_all(x, ("y", "pair"), 0, 0, tiled=True)


def body(acts, cotangent, gates, owners, slots, w_in, w_out):
    index = lax.axis_index("segment")
    top = index == 1
    core = index.astype(I32).reshape(1)
    own_in, own_out = w_in[0, 0], w_out[0, 0]
    other_in = lax.ppermute(own_in, "segment", SWAP)
    other_out = lax.ppermute(own_out, "segment", SWAP)
    weights = (own_in, other_in, own_out, other_out)

    table = (2, 2, TOK)
    (packed,) = call(
        start_kernel, [SM] + [HB] * 5, [(3 * ALL, LOW)], "start",
        [pltpu.VMEM((3, TOK, SHARE), BF), pltpu.VMEM(table, F32), pltpu.VMEM(table, I32),
         pltpu.VMEM(table, I32), pltpu.SemaphoreType.DMA((6,))], mib=60,
    )(core, acts, cotangent, gates, owners, slots)
    (sent,) = call(functools.partial(spread_kernel, 3), [VM], [(NY * NX, 3 * YROWS, LOW)], "spread3", mib=16)(
        over_z(packed)
    )
    saved = over_yx(sent)
    blocks, wide = (NY * NX, YROWS, LOW), (NY * NZ * CAP, WIDTH)
    parts, *kept1 = call(upper_kernel, [SM] + [VM] * 5, [blocks] + [wide] * 4, "upper")(core, saved, *weights)
    (rows,) = call(gather_kernel, [VM], [(ALL, LOW)], "gather")(over_yx(parts))
    res1, packed = call(middle_kernel, [SM] + [VM] * 5, [(TOK, SHARE), (ALL, LOW)], "middle")(
        core, over_z(rows), cotangent, gates, owners, slots
    )
    (sent,) = call(functools.partial(spread_kernel, 1), [VM], [(NY * NX, YROWS, LOW)], "spread1")(
        over_z(packed)
    )
    parts, *keep, give = call(
        lower_kernel, [SM] + [VM] * 10, [blocks] + [wide] * 4 + [(4,) + wide], "lower",
        [pltpu.VMEM((4,) + wide, BF), pltpu.SemaphoreType.DMA((4,))], places=[VM] * 5 + [HB],
    )(core, saved, over_yx(sent), *kept1, *weights)
    came = lax.ppermute(give, "segment", SWAP)
    (rows,) = call(gather_kernel, [VM], [(ALL, LOW)], "gather")(over_yx(parts))

    grad_in, grad_out, mark = call(
        weight_kernel, [HB] * 5, [(WIDTH, HID), (HID, WIDTH), (16, 128)], "weight",
        [pltpu.VMEM((4, 2 * NY * NZ * CAP, WIDTH), BF), pltpu.VMEM((2, WIDTH, HID), BF), pltpu.SemaphoreType.DMA((10,))],
        mib=16, cost=(2 * 10**9, 6 * 10**6), places=[HB, HB, VM],
    )(*keep, came)
    mine, other = call(end_kernel, [SM] + [VM] * 5, [(TOK, SHARE)] * 2, "end")(
        core, over_z(rows), res1, owners, slots, mark
    )
    got = lax.ppermute(other, "segment", SWAP)
    grads = jnp.stack([jnp.where(top, got, mine), jnp.where(top, mine, got)])
    return grads[None], grad_in[None, None], grad_out[None, None]


def solution(mesh):
    fine = Mesh(mesh.devices.reshape(2, NY, NZ, NX), ("segment", "y", "z", "pair"))
    e = ("y", "z")
    placed = (
        P(None, None, e, "pair"),
        P(None, e, "pair"),
        P(None, None, e),
        P(None, None, e),
        P(None, None, e),
        P("segment", e, None, "pair"),
        P("segment", e, "pair", None),
    )
    return jax.shard_map(
        body,
        mesh=fine,
        in_specs=placed,
        out_specs=(
            P("segment", None, e, "pair"),
            P("segment", e, None, "pair"),
            P("segment", e, "pair", None),
        ),
        check_vma=False,
    )
```

```python
import functools

import jax
import jax.numpy as jnp
from jax import lax
from jax.experimental import pallas as pl
from jax.experimental.pallas import tpu as pltpu
from jax.sharding import Mesh, PartitionSpec as P

BF = jnp.bfloat16
F32 = jnp.float32
I32 = jnp.int32
SWAP = [(0, 1), (1, 0)]

NY, NZ, NX = 4, 16, 4
CAP = 4
TOK = 192
SHARE = 192
WIDTH = SHARE * NX
FIRST = NZ // 2
HID = 768
LOW = 128
ZROWS = NY * CAP + NY * CAP // 2
YROWS = NZ * CAP + NZ * CAP // 2
ALL = NZ * ZROWS


def dot(a, b, ca=1, cb=0):
    return lax.dot_general(a, b, (((ca,), (cb,)), ((), ())), preferred_element_type=F32)


def hot(cond):
    return jnp.where(cond, 1.0, 0.0).astype(BF)


def iota(shape, dim):
    return lax.broadcasted_iota(I32, shape, dim)


def column(row):
    n = row.shape[1]
    eye = iota((n, n), 0) == iota((n, n), 1)
    return jnp.sum(jnp.where(eye, row.astype(F32), 0.0), axis=1, keepdims=True)


def targets(owner, slot):
    base = ((owner + FIRST) & (NZ - 1)) * ZROWS
    y = owner >> 4
    return base + y * CAP + slot, base + NY * CAP + y * 2 + (slot >> 1), slot & 1


def pack(values, owner, slot):
    low_at, high_at, odd = targets(owner, slot)
    at = iota((ALL, TOK), 0)
    low = hot(at == low_at)
    even_hot = hot((at == high_at) & (odd == 0))
    odd_hot = hot((at == high_at) & (odd == 1))
    out = []
    for v in values:
        high = v[:, LOW:]
        none = jnp.zeros_like(high)
        out.append(
            dot(low, v[:, :LOW])
            + dot(even_hot, jnp.concatenate([high, none], axis=1))
            + dot(odd_hot, jnp.concatenate([none, high], axis=1))
        )
    return out


def unpack(rows, owner, slot):
    low_at, high_at, odd = (column(t).astype(I32) for t in targets(owner, slot))
    at = iota((TOK, ALL), 1)
    low = dot(hot(at == low_at), rows)
    even_rows = dot(hot((at == high_at) & (odd == 0)), rows)
    odd_rows = dot(hot((at == high_at) & (odd == 1)), rows)
    high = even_rows[:, : SHARE - LOW] + odd_rows[:, SHARE - LOW :]
    return jnp.concatenate([low, high], axis=1)


def row_of(ref, layer, core):
    return jnp.where(core == 0, ref[layer, 0:1, :], ref[layer, 1:2, :])


def start_kernel(core_ref, acts, cot, gates, owners, slots, out, tok, gate_v, owner_v, slot_v, sems):
    core = core_ref[0]
    copies = [
        pltpu.make_async_copy(src, dst, sems.at[k])
        for k, (src, dst) in enumerate(
            [
                (owners, owner_v),
                (slots, slot_v),
                (gates, gate_v),
                (cot.at[core], tok.at[0]),
                (acts.at[1, core], tok.at[1]),
                (acts.at[0, core], tok.at[2]),
            ]
        )
    ]
    for copy in copies:
        copy.start()
    for copy in copies:
        copy.wait()
    gate = column(row_of(gate_v, 1, core))
    scaled = (gate * tok[0].astype(F32)).astype(BF)
    first = pack([tok[1], scaled], row_of(owner_v, 1, core), row_of(slot_v, 1, core))
    second = pack([tok[2]], row_of(owner_v, 0, core), row_of(slot_v, 0, core))
    parts = [p.reshape(NZ, ZROWS, LOW) for p in first + second]
    out[...] = jnp.concatenate(parts, axis=1).reshape(3 * ALL, LOW).astype(BF)


def spread_kernel(count, rows, out):
    shape = (NY, YROWS, ALL)
    y, k, at = iota(shape, 0), iota(shape, 1), iota(shape, 2)
    z = (k & 31) >> 1
    half = k & 1
    low = z * ZROWS + y * CAP + half * 2 + (k >> 5)
    high = z * ZROWS + NY * CAP + y * 2 + half
    move = hot((at == jnp.where(k < NZ * CAP, low, high)).reshape(ALL, ALL))
    value = rows[...].astype(F32).reshape(NZ, count * ZROWS, LOW)
    for a in range(count):
        part = value[:, a * ZROWS : (a + 1) * ZROWS].reshape(ALL, LOW).astype(BF)
        moved = dot(move, part).astype(BF)
        for j in range(NY):
            for i in range(NX):
                out[j * NX + i, a * YROWS : (a + 1) * YROWS, :] = moved[j * YROWS : (j + 1) * YROWS]


def gather_kernel(parts, out):
    shape = (NZ, ZROWS, ALL)
    z, k, at = iota(shape, 0), iota(shape, 1), iota(shape, 2)
    low = (k >> 2) * YROWS + (k & 1) * 32 + z * 2 + ((k & 3) >> 1)
    k2 = k - NY * CAP
    high = (k2 >> 1) * YROWS + NZ * CAP + z * 2 + (k2 & 1)
    move = hot((at == jnp.where(k < NY * CAP, low, high)).reshape(ALL, ALL))
    sums = []
    for j in range(NY):
        total = parts[j * NX].astype(F32)
        for i in range(1, NX):
            total = total + parts[j * NX + i].astype(F32)
        sums.append(total)
    out[...] = dot(move, jnp.concatenate(sums, axis=0).astype(BF)).astype(BF)


def assemble(ref, first):
    rows = []
    for j in range(NY):
        cols = []
        for i in range(NX):
            low = ref[j * NX + i, first : first + 64, :]
            high = ref[j * NX + i, first + 64 : first + YROWS, :]
            cols.append(low)
            cols.append(jnp.concatenate([high[:, :64], high[:, 64:]], axis=0))
        rows.append(jnp.concatenate(cols, axis=1))
    return jnp.concatenate(rows, axis=0)


def expert_step(x, grad, w_in, w_out, out, save):
    save(3, grad)
    inv = lax.rsqrt(jnp.mean(x * x, axis=1, keepdims=True) + 1e-06)
    normed = (x * inv).astype(BF)
    save(0, normed)
    u = dot(normed, w_in())
    square = u * u
    s = jnp.tanh(0.7978845608 * (u + 0.044715 * square * u))
    save(2, (0.5 * u * (1.0 + s)).astype(BF))
    slope = 0.5 * (1.0 + s) + 0.5 * u * (1.0 - s * s) * 0.7978845608 * (1.0 + 0.134145 * square)
    back = (dot(grad, w_out(), 1, 1) * slope).astype(BF)
    save(1, back)
    part = dot(back, w_in(), 1, 1)
    inner = jnp.sum(part * x, axis=1, keepdims=True)
    branch = (inv * part - (inv * inv * inv * inner * (1.0 / WIDTH)) * x).astype(BF)
    for j in range(NY):
        for i in range(NX):
            at = i * SHARE
            block = branch[j * 64 : (j + 1) * 64]
            out[j * NX + i, 0:64, :] = block[:, at : at + LOW]
            out[j * NX + i, 64:YROWS, :] = jnp.concatenate(
                [block[:32, at + LOW : at + SHARE], block[32:, at + LOW : at + SHARE]], axis=1
            )


def held(ref):
    return lambda: ref[...]


def fetched(source, buffer, sem):
    copy = pltpu.make_async_copy(source, buffer, sem)
    copy.start()
    pending = [copy]

    def value():
        if pending:
            pending.pop().wait()
        return buffer[...]

    return value


def upper_kernel(core_ref, saved, own_in, other_in, own_out, other_out, out, k0, k1, k2, k3, in_buf, out_buf, sems):
    def run(w_in, w_out):
        def save(k, value):
            (k0, k1, k2, k3)[k][...] = value

        expert_step(assemble(saved, 0).astype(F32), assemble(saved, YROWS), w_in, w_out, out, save)

    @pl.when(core_ref[0] == 1)
    def _():
        run(held(own_in), held(own_out))

    @pl.when(core_ref[0] != 1)
    def _():
        run(fetched(other_in, in_buf, sems.at[0]), fetched(other_out, out_buf, sems.at[1]))


def lower_kernel(
    core_ref, saved, came, n1, b1, h1, g1, own_in, other_in, own_out, other_out,
    out, k0, k1, k2, k3, give, kept, in_buf, out_buf, sems,
):
    keep, above = (k0, k1, k2, k3), (n1, b1, h1, g1)

    def run(w_in, w_out, save):
        expert_step(assemble(saved, 2 * YROWS).astype(F32), assemble(came, 0), w_in, w_out, out, save)

    @pl.when(core_ref[0] == 0)
    def _():
        copies = [pltpu.make_async_copy(above[k], give.at[k], sems.at[k]) for k in range(4)]
        for copy in copies:
            copy.start()

        def save(k, value):
            keep[k][...] = value

        run(held(own_in), held(own_out), save)
        for copy in copies:
            copy.wait()

    @pl.when(core_ref[0] != 0)
    def _():
        w_in, w_out = fetched(other_in, in_buf, sems.at[4]), fetched(other_out, out_buf, sems.at[5])
        copies = [pltpu.make_async_copy(kept.at[k], give.at[k], sems.at[k]) for k in range(4)]

        def save(k, value):
            kept[k] = value
            copies[k].start()
            keep[k][...] = above[k][...]

        run(w_in, w_out, save)
        for copy in copies:
            copy.wait()


def weight_kernel(k0, k1, k2, k3, came, first, second, mark, rows, sums, sems):
    half = NY * NZ * CAP
    loads = [
        [pltpu.make_async_copy(src, rows.at[k, n * half : (n + 1) * half], sems.at[2 * k + n])
         for n, src in enumerate([(k0, k1, k2, k3)[k], came.at[k]])]
        for k in range(4)
    ]
    for pair in loads:
        for copy in pair:
            copy.start()

    def product(k, at, dst):
        for copy in loads[k] + loads[k + 1]:
            copy.wait()
        sums[at] = dot(rows[k], rows[k + 1], 0, 0).astype(BF)
        copy = pltpu.make_async_copy(sums.at[at], dst, sems.at[8 + at])
        copy.start()
        return copy

    stores = [product(0, 0, first), product(2, 1, second)]
    mark[0] = 0
    for copy in stores:
        copy.wait()


def middle_kernel(core_ref, rows, cot, gates, owners, slots, result, out):
    core = core_ref[0]
    branch = unpack(rows[...], row_of(owners, 1, core), row_of(slots, 1, core))
    res = (cot[core].astype(F32) + branch).astype(BF)
    result[...] = res
    gate = column(row_of(gates, 0, core))
    scaled = (gate * res.astype(F32)).astype(BF)
    (packed,) = pack([scaled], row_of(owners, 0, core), row_of(slots, 0, core))
    out[...] = packed.astype(BF)


def end_kernel(core_ref, rows, above, owners, slots, mark, keep, give):
    core = core_ref[0]
    branch = unpack(rows[...], row_of(owners, 0, core), row_of(slots, 0, core))
    res = (above[...].astype(F32) + branch).astype(BF)
    keep[...] = jnp.where(core == 0, res, above[...])
    give[...] = jnp.where(core == 0, above[...], res)


VM = pl.BlockSpec(memory_space=pltpu.VMEM)
SM = pl.BlockSpec(memory_space=pltpu.SMEM)
HB = pl.BlockSpec(memory_space=pltpu.HBM)


def call(kernel, ins, outs, name, scratch=(), mib=16, cost=None, places=None):
    return pl.pallas_call(
        kernel,
        in_specs=list(ins),
        out_specs=places or [VM] * len(outs),
        out_shape=[o if hasattr(o, "dtype") else jax.ShapeDtypeStruct(o, BF) for o in outs],
        scratch_shapes=list(scratch),
        compiler_params=pltpu.CompilerParams(vmem_limit_bytes=mib << 20),
        cost_estimate=cost and pl.CostEstimate(flops=cost[0], bytes_accessed=cost[1], transcendentals=0),
        name=name,
    )


def over_z(x):
    ring = [[(FIRST + k) % NZ for k in range(NZ)]]
    x = x.reshape(NZ, -1, LOW)
    return lax.all_to_all(x, "z", 0, 0, axis_index_groups=ring, tiled=True).reshape(-1, LOW)


def over_yx(x):
    return lax.all_to_all(x, ("y", "pair"), 0, 0, tiled=True)


def body(acts, cotangent, gates, owners, slots, w_in, w_out):
    index = lax.axis_index("segment")
    top = index == 1
    core = index.astype(I32).reshape(1)
    own_in, own_out = w_in[0, 0], w_out[0, 0]
    other_in = lax.ppermute(own_in, "segment", SWAP)
    other_out = lax.ppermute(own_out, "segment", SWAP)
    weights = (own_in, other_in, own_out, other_out)

    table = (2, 2, TOK)
    (packed,) = call(
        start_kernel, [SM] + [HB] * 5, [(3 * ALL, LOW)], "start",
        [pltpu.VMEM((3, TOK, SHARE), BF), pltpu.VMEM(table, F32), pltpu.VMEM(table, I32),
         pltpu.VMEM(table, I32), pltpu.SemaphoreType.DMA((6,))], mib=60,
    )(core, acts, cotangent, gates, owners, slots)
    (sent,) = call(functools.partial(spread_kernel, 3), [VM], [(NY * NX, 3 * YROWS, LOW)], "spread3", mib=16)(
        over_z(packed)
    )
    saved = over_yx(sent)
    blocks, wide = (NY * NX, YROWS, LOW), (NY * NZ * CAP, WIDTH)
    parts, *kept1 = call(
        upper_kernel, [SM, VM] + [VM, HB] * 2, [blocks] + [wide] * 4, "upper",
        [pltpu.VMEM((WIDTH, HID), BF), pltpu.VMEM((HID, WIDTH), BF), pltpu.SemaphoreType.DMA((2,))],
    )(core, saved, *weights)
    (rows,) = call(gather_kernel, [VM], [(ALL, LOW)], "gather")(over_yx(parts))
    res1, packed = call(middle_kernel, [SM] + [VM] * 5, [(TOK, SHARE), (ALL, LOW)], "middle")(
        core, over_z(rows), cotangent, gates, owners, slots
    )
    (sent,) = call(functools.partial(spread_kernel, 1), [VM], [(NY * NX, YROWS, LOW)], "spread1")(
        over_z(packed)
    )
    parts, *keep, give = call(
        lower_kernel, [SM] + [VM] * 6 + [VM, HB] * 2, [blocks] + [wide] * 4 + [(4,) + wide], "lower",
        [pltpu.VMEM((4,) + wide, BF), pltpu.VMEM((WIDTH, HID), BF), pltpu.VMEM((HID, WIDTH), BF),
         pltpu.SemaphoreType.DMA((6,))], places=[VM] * 5 + [HB],
    )(core, saved, over_yx(sent), *kept1, *weights)
    came = lax.ppermute(give, "segment", SWAP)
    (rows,) = call(gather_kernel, [VM], [(ALL, LOW)], "gather")(over_yx(parts))

    grad_in, grad_out, mark = call(
        weight_kernel, [HB] * 5, [(WIDTH, HID), (HID, WIDTH), jax.ShapeDtypeStruct((1,), I32)], "weight",
        [pltpu.VMEM((4, 2 * NY * NZ * CAP, WIDTH), BF), pltpu.VMEM((2, WIDTH, HID), BF), pltpu.SemaphoreType.DMA((10,))],
        mib=56, cost=(2 * 10**9, 6 * 10**6), places=[HB, HB, SM],
    )(*keep, came)
    mine, other = call(end_kernel, [SM] + [VM] * 4 + [SM], [(TOK, SHARE)] * 2, "end")(
        core, over_z(rows), res1, owners, slots, mark
    )
    got = lax.ppermute(other, "segment", SWAP)
    grads = jnp.stack([jnp.where(top, got, mine), jnp.where(top, mine, got)])
    return grads[None], grad_in[None, None], grad_out[None, None]


def solution(mesh):
    fine = Mesh(mesh.devices.reshape(2, NY, NZ, NX), ("segment", "y", "z", "pair"))
    e = ("y", "z")
    placed = (
        P(None, None, e, "pair"),
        P(None, e, "pair"),
        P(None, None, e),
        P(None, None, e),
        P(None, None, e),
        P("segment", e, None, "pair"),
        P("segment", e, "pair", None),
    )
    return jax.shard_map(
        body,
        mesh=fine,
        in_specs=placed,
        out_specs=(
            P("segment", None, e, "pair"),
            P("segment", e, None, "pair"),
            P("segment", e, "pair", None),
        ),
        check_vma=False,
    )
```

```python
import functools

import jax
import jax.numpy as jnp
from jax import lax
from jax.experimental import pallas as pl
from jax.experimental.pallas import tpu as pltpu
from jax.sharding import Mesh, PartitionSpec as P

BF = jnp.bfloat16
F32 = jnp.float32
I32 = jnp.int32
SWAP = [(0, 1), (1, 0)]

NY, NZ, NX = 4, 16, 4
CAP = 4
TOK = 192
SHARE = 192
WIDTH = SHARE * NX
FIRST = NZ // 2
HID = 768
LOW = 128
ZROWS = NY * CAP + NY * CAP // 2
YROWS = NZ * CAP + NZ * CAP // 2
CUTS = 4
ALL = NZ * ZROWS


def dot(a, b, ca=1, cb=0):
    return lax.dot_general(a, b, (((ca,), (cb,)), ((), ())), preferred_element_type=F32)


def hot(cond):
    return jnp.where(cond, 1.0, 0.0).astype(BF)


def iota(shape, dim):
    return lax.broadcasted_iota(I32, shape, dim)


def column(row):
    n = row.shape[1]
    eye = iota((n, n), 0) == iota((n, n), 1)
    return jnp.sum(jnp.where(eye, row.astype(F32), 0.0), axis=1, keepdims=True)


def targets(owner, slot):
    base = ((owner + FIRST) & (NZ - 1)) * ZROWS
    y = owner >> 4
    return base + y * CAP + slot, base + NY * CAP + y * 2 + (slot >> 1), slot & 1


def routes(owner, slot):
    low_at, high_at, odd = targets(owner, slot)
    at = iota((ALL, TOK), 0)
    low = hot(at == low_at)
    even_hot = hot((at == high_at) & (odd == 0))
    odd_hot = hot((at == high_at) & (odd == 1))
    return low, even_hot, odd_hot


def pack(values, hots):
    low, even_hot, odd_hot = hots
    out = []
    for v in values:
        high = v[:, LOW:]
        none = jnp.zeros_like(high)
        out.append(
            dot(low, v[:, :LOW])
            + dot(even_hot, jnp.concatenate([high, none], axis=1))
            + dot(odd_hot, jnp.concatenate([none, high], axis=1))
        )
    return out


def unpack(rows, owner, slot):
    low_at, high_at, odd = (column(t).astype(I32) for t in targets(owner, slot))
    at = iota((TOK, ALL), 1)
    low = dot(hot(at == low_at), rows)
    even_rows = dot(hot((at == high_at) & (odd == 0)), rows)
    odd_rows = dot(hot((at == high_at) & (odd == 1)), rows)
    high = even_rows[:, : SHARE - LOW] + odd_rows[:, SHARE - LOW :]
    return jnp.concatenate([low, high], axis=1)


def row_of(ref, layer, core):
    return jnp.where(core == 0, ref[layer, 0:1, :], ref[layer, 1:2, :])


def start_kernel(core_ref, acts, cot, gates, owners, slots, out, tok, gate_v, owner_v, slot_v, sems):
    core = core_ref[0]
    copies = [
        pltpu.make_async_copy(src, dst, sems.at[k])
        for k, (src, dst) in enumerate(
            [
                (owners, owner_v),
                (slots, slot_v),
                (gates, gate_v),
                (cot.at[core], tok.at[0]),
                (acts.at[1, core], tok.at[1]),
                (acts.at[0, core], tok.at[2]),
            ]
        )
    ]
    for copy in copies:
        copy.start()
    copies[0].wait()
    copies[1].wait()
    upper = routes(row_of(owner_v, 1, core), row_of(slot_v, 1, core))
    lower = routes(row_of(owner_v, 0, core), row_of(slot_v, 0, core))
    for copy in copies[2:]:
        copy.wait()
    gate = column(row_of(gate_v, 1, core))
    scaled = (gate * tok[0].astype(F32)).astype(BF)
    first = pack([tok[1], scaled], upper)
    second = pack([tok[2]], lower)
    parts = [p.reshape(NZ, ZROWS, LOW) for p in first + second]
    out[...] = jnp.concatenate(parts, axis=1).reshape(3 * ALL, LOW).astype(BF)


def spread_move():
    shape = (NY, YROWS, ALL)
    y, k, at = iota(shape, 0), iota(shape, 1), iota(shape, 2)
    z = (k & 31) >> 1
    half = k & 1
    low = z * ZROWS + y * CAP + half * 2 + (k >> 5)
    high = z * ZROWS + NY * CAP + y * 2 + half
    return hot((at == jnp.where(k < NZ * CAP, low, high)).reshape(ALL, ALL))


def spread_kernel(rows, out):
    moved = dot(spread_move(), rows[...]).astype(BF)
    for j in range(NY):
        for i in range(NX):
            out[j * NX + i] = moved[j * YROWS : (j + 1) * YROWS]


def spread3_kernel(rows, out, moved, sems):
    move = spread_move()
    value = rows[...].astype(F32).reshape(NZ, 3 * ZROWS, LOW)
    copies = []
    for a in range(3):
        part = value[:, a * ZROWS : (a + 1) * ZROWS].reshape(ALL, LOW).astype(BF)
        moved[a] = dot(move, part).astype(BF).reshape(NY, YROWS, LOW)
        for i in range(NX):
            copy = pltpu.make_async_copy(moved.at[a], out.at[:, i, a * YROWS : (a + 1) * YROWS], sems.at[a, i])
            copy.start()
            copies.append(copy)
    for copy in copies:
        copy.wait()


def gather_kernel(parts, out):
    shape = (NZ, ZROWS, ALL)
    z, k, at = iota(shape, 0), iota(shape, 1), iota(shape, 2)
    low = (k >> 2) * YROWS + (k & 1) * 32 + z * 2 + ((k & 3) >> 1)
    k2 = k - NY * CAP
    high = (k2 >> 1) * YROWS + NZ * CAP + z * 2 + (k2 & 1)
    move = hot((at == jnp.where(k < NY * CAP, low, high)).reshape(ALL, ALL))
    sums = []
    for j in range(NY):
        total = parts[j * NX].astype(F32)
        for i in range(1, NX):
            total = total + parts[j * NX + i].astype(F32)
        sums.append(total)
    out[...] = dot(move, jnp.concatenate(sums, axis=0).astype(BF)).astype(BF)


def assemble(ref, first):
    rows = []
    for j in range(NY):
        cols = []
        for i in range(NX):
            low = ref[j * NX + i, first : first + 64, :]
            high = ref[j * NX + i, first + 64 : first + YROWS, :]
            cols.append(low)
            cols.append(jnp.concatenate([high[:, :64], high[:, 64:]], axis=0))
        rows.append(jnp.concatenate(cols, axis=1))
    return jnp.concatenate(rows, axis=0)


def expert_step(x, grad, w_in, w_out, out, save):
    save(3, grad)
    inv = lax.rsqrt(jnp.mean(x * x, axis=1, keepdims=True) + 1e-06)
    normed = (x * inv).astype(BF)
    save(0, normed)
    u = dot(normed, w_in())
    square = u * u
    s = jnp.tanh(0.7978845608 * (u + 0.044715 * square * u))
    save(2, (0.5 * u * (1.0 + s)).astype(BF))
    slope = 0.5 * (1.0 + s) + 0.5 * u * (1.0 - s * s) * 0.7978845608 * (1.0 + 0.134145 * square)
    back = (dot(grad, w_out(), 1, 1) * slope).astype(BF)
    save(1, back)
    part = dot(back, w_in(), 1, 1)
    inner = jnp.sum(part * x, axis=1, keepdims=True)
    branch = (inv * part - (inv * inv * inv * inner * (1.0 / WIDTH)) * x).astype(BF)
    for j in range(NY):
        for i in range(NX):
            at = i * SHARE
            block = branch[j * 64 : (j + 1) * 64]
            out[j * NX + i, 0:64, :] = block[:, at : at + LOW]
            out[j * NX + i, 64:YROWS, :] = jnp.concatenate(
                [block[:32, at + LOW : at + SHARE], block[32:, at + LOW : at + SHARE]], axis=1
            )


def held(ref):
    return lambda: ref[...]


def fetched(source, buffer, sems):
    step = WIDTH // CUTS
    copies = [
        pltpu.make_async_copy(source.at[k * step : (k + 1) * step], buffer.at[k * step : (k + 1) * step], sems.at[k])
        for k in range(CUTS)
    ]
    for copy in copies:
        copy.start()

    def value():
        while copies:
            copies.pop(0).wait()
        return buffer[...]

    return value


def upper_kernel(core_ref, saved, own_in, other_in, own_out, other_out, out, k0, k1, k2, k3, in_buf, out_buf, sems):
    def run(w_in, w_out):
        def save(k, value):
            (k0, k1, k2, k3)[k][...] = value

        expert_step(assemble(saved, 0).astype(F32), assemble(saved, YROWS), w_in, w_out, out, save)

    @pl.when(core_ref[0] == 1)
    def _():
        run(held(own_in), held(own_out))

    @pl.when(core_ref[0] != 1)
    def _():
        run(fetched(other_in, in_buf, sems.at[0]), fetched(other_out, out_buf, sems.at[1]))


def lower_kernel(
    core_ref, saved, came, n1, b1, h1, g1, own_in, other_in, own_out, other_out,
    out, k0, k1, k2, k3, give, kept, in_buf, out_buf, sems, more,
):
    keep, above = (k0, k1, k2, k3), (n1, b1, h1, g1)

    def run(w_in, w_out, save):
        expert_step(assemble(saved, 2 * YROWS).astype(F32), assemble(came, 0), w_in, w_out, out, save)

    @pl.when(core_ref[0] == 0)
    def _():
        copies = [pltpu.make_async_copy(above[k], give.at[k], sems.at[k]) for k in range(4)]
        for copy in copies:
            copy.start()

        def save(k, value):
            keep[k][...] = value

        run(held(own_in), held(own_out), save)
        for copy in copies:
            copy.wait()

    @pl.when(core_ref[0] != 0)
    def _():
        w_in, w_out = fetched(other_in, in_buf, more.at[0]), fetched(other_out, out_buf, more.at[1])
        copies = [pltpu.make_async_copy(kept.at[k], give.at[k], sems.at[k]) for k in range(4)]

        def save(k, value):
            kept[k] = value
            copies[k].start()
            keep[k][...] = above[k][...]

        run(w_in, w_out, save)
        for copy in copies:
            copy.wait()


def weight_kernel(k0, k1, k2, k3, came, first, second, rows, sums, sems):
    half = NY * NZ * CAP
    loads = [
        [pltpu.make_async_copy(src, rows.at[k, n * half : (n + 1) * half], sems.at[2 * k + n])
         for n, src in enumerate([(k0, k1, k2, k3)[k], came.at[k]])]
        for k in range(4)
    ]
    for pair in loads:
        for copy in pair:
            copy.start()

    def product(k, at, dst):
        for copy in loads[k] + loads[k + 1]:
            copy.wait()
        sums[at] = dot(rows[k], rows[k + 1], 0, 0).astype(BF)
        copy = pltpu.make_async_copy(sums.at[at], dst, sems.at[8 + at])
        copy.start()
        return copy

    stores = [product(0, 0, first), product(2, 1, second)]
    for copy in stores:
        copy.wait()


def middle_kernel(core_ref, rows, cot, gates, owners, slots, result, out):
    core = core_ref[0]
    branch = unpack(rows[...], row_of(owners, 1, core), row_of(slots, 1, core))
    res = (cot[core].astype(F32) + branch).astype(BF)
    result[...] = res
    gate = column(row_of(gates, 0, core))
    scaled = (gate * res.astype(F32)).astype(BF)
    (packed,) = pack([scaled], routes(row_of(owners, 0, core), row_of(slots, 0, core)))
    out[...] = packed.astype(BF)


def end_kernel(core_ref, rows, above, owners, slots, grad_in, keep, give, same):
    core = core_ref[0]
    branch = unpack(rows[...], row_of(owners, 0, core), row_of(slots, 0, core))
    res = (above[...].astype(F32) + branch).astype(BF)
    keep[...] = jnp.where(core == 0, res, above[...])
    give[...] = jnp.where(core == 0, above[...], res)


VM = pl.BlockSpec(memory_space=pltpu.VMEM)
SM = pl.BlockSpec(memory_space=pltpu.SMEM)
HB = pl.BlockSpec(memory_space=pltpu.HBM)


def call(kernel, ins, outs, name, scratch=(), mib=16, cost=None, places=None, alias=None):
    return pl.pallas_call(
        kernel,
        in_specs=list(ins),
        out_specs=places or [VM] * len(outs),
        out_shape=[o if hasattr(o, "dtype") else jax.ShapeDtypeStruct(o, BF) for o in outs],
        scratch_shapes=list(scratch),
        compiler_params=pltpu.CompilerParams(vmem_limit_bytes=mib << 20),
        cost_estimate=cost and pl.CostEstimate(flops=cost[0], bytes_accessed=cost[1], transcendentals=0),
        input_output_aliases=alias or {},
        name=name,
    )


def over_z(x):
    ring = [[(FIRST + k) % NZ for k in range(NZ)]]
    x = x.reshape(NZ, -1, LOW)
    return lax.all_to_all(x, "z", 0, 0, axis_index_groups=ring, tiled=True).reshape(-1, LOW)


def over_yx(x):
    return lax.all_to_all(x, ("y", "pair"), 0, 0, tiled=True)


def body(acts, cotangent, gates, owners, slots, w_in, w_out):
    index = lax.axis_index("segment")
    top = index == 1
    core = index.astype(I32).reshape(1)
    own_in, own_out = w_in[0, 0], w_out[0, 0]
    other_in = lax.ppermute(own_in, "segment", SWAP)
    other_out = lax.ppermute(own_out, "segment", SWAP)
    weights = (own_in, other_in, own_out, other_out)

    table = (2, 2, TOK)
    (packed,) = call(
        start_kernel, [SM] + [HB] * 5, [(3 * ALL, LOW)], "start",
        [pltpu.VMEM((3, TOK, SHARE), BF), pltpu.VMEM(table, F32), pltpu.VMEM(table, I32),
         pltpu.VMEM(table, I32), pltpu.SemaphoreType.DMA((6,))], mib=60,
    )(core, acts, cotangent, gates, owners, slots)
    (sent,) = call(
        spread3_kernel, [VM], [(NY, NX, 3 * YROWS, LOW)], "spread3",
        [pltpu.VMEM((3, NY, YROWS, LOW), BF), pltpu.SemaphoreType.DMA((3, NX))], places=[HB],
    )(over_z(packed))
    saved = over_yx(sent.reshape(NY * NX, 3 * YROWS, LOW))
    blocks, wide = (NY * NX, YROWS, LOW), (NY * NZ * CAP, WIDTH)
    parts, *kept1 = call(
        upper_kernel, [SM, VM] + [VM, HB] * 2, [blocks] + [wide] * 4, "upper",
        [pltpu.VMEM((WIDTH, HID), BF), pltpu.VMEM((HID, WIDTH), BF), pltpu.SemaphoreType.DMA((2, CUTS))],
    )(core, saved, *weights)
    (rows,) = call(gather_kernel, [VM], [(ALL, LOW)], "gather")(over_yx(parts))
    res1, packed = call(middle_kernel, [SM] + [VM] * 5, [(TOK, SHARE), (ALL, LOW)], "middle")(
        core, over_z(rows), cotangent, gates, owners, slots
    )
    (sent,) = call(spread_kernel, [VM], [(NY * NX, YROWS, LOW)], "spread1")(
        over_z(packed)
    )
    parts, *keep, give = call(
        lower_kernel, [SM] + [VM] * 6 + [VM, HB] * 2, [blocks] + [wide] * 4 + [(4,) + wide], "lower",
        [pltpu.VMEM((4,) + wide, BF), pltpu.VMEM((WIDTH, HID), BF), pltpu.VMEM((HID, WIDTH), BF),
         pltpu.SemaphoreType.DMA((4,)), pltpu.SemaphoreType.DMA((2, CUTS))], places=[VM] * 5 + [HB],
    )(core, saved, over_yx(sent), *kept1, *weights)
    came = lax.ppermute(give, "segment", SWAP)
    (rows,) = call(gather_kernel, [VM], [(ALL, LOW)], "gather")(over_yx(parts))

    grad_in, grad_out = call(
        weight_kernel, [HB] * 5, [(WIDTH, HID), (HID, WIDTH)], "weight",
        [pltpu.VMEM((4, 2 * NY * NZ * CAP, WIDTH), BF), pltpu.VMEM((2, WIDTH, HID), BF), pltpu.SemaphoreType.DMA((10,))],
        mib=56, cost=(2 * 10**9, 6 * 10**6), places=[HB, HB],
    )(*keep, came)
    mine, other, grad_in = call(
        end_kernel, [SM] + [VM] * 4 + [HB], [(TOK, SHARE)] * 2 + [(WIDTH, HID)], "end",
        places=[VM, VM, HB], alias={5: 2},
    )(core, over_z(rows), res1, owners, slots, grad_in)
    got = lax.ppermute(other, "segment", SWAP)
    grads = jnp.stack([jnp.where(top, got, mine), jnp.where(top, mine, got)])
    return grads[None], grad_in[None, None], grad_out[None, None]


def solution(mesh):
    fine = Mesh(mesh.devices.reshape(2, NY, NZ, NX), ("segment", "y", "z", "pair"))
    e = ("y", "z")
    placed = (
        P(None, None, e, "pair"),
        P(None, e, "pair"),
        P(None, None, e),
        P(None, None, e),
        P(None, None, e),
        P("segment", e, None, "pair"),
        P("segment", e, "pair", None),
    )
    return jax.shard_map(
        body,
        mesh=fine,
        in_specs=placed,
        out_specs=(
            P("segment", None, e, "pair"),
            P("segment", e, None, "pair"),
            P("segment", e, "pair", None),
        ),
        check_vma=False,
    )
```

```python
import functools

import jax
import jax.numpy as jnp
from jax import lax
from jax.experimental import pallas as pl
from jax.experimental.pallas import tpu as pltpu
from jax.sharding import Mesh, PartitionSpec as P

BF = jnp.bfloat16
F32 = jnp.float32
I32 = jnp.int32
SWAP = [(0, 1), (1, 0)]

NY, NZ, NX = 4, 16, 4
CAP = 4
TOK = 192
SHARE = 192
WIDTH = SHARE * NX
FIRST = NZ // 2
HID = 768
LOW = 128
ZROWS = NY * CAP + NY * CAP // 2
YROWS = NZ * CAP + NZ * CAP // 2
CUTS = 4
ALL = NZ * ZROWS


def dot(a, b, ca=1, cb=0):
    return lax.dot_general(a, b, (((ca,), (cb,)), ((), ())), preferred_element_type=F32)


def hot(cond):
    return jnp.where(cond, 1.0, 0.0).astype(BF)


def iota(shape, dim):
    return lax.broadcasted_iota(I32, shape, dim)


def column(row):
    n = row.shape[1]
    eye = iota((n, n), 0) == iota((n, n), 1)
    return jnp.sum(jnp.where(eye, row.astype(F32), 0.0), axis=1, keepdims=True)


def targets(owner, slot):
    base = ((owner + FIRST) & (NZ - 1)) * ZROWS
    y = owner >> 4
    return base + y * CAP + slot, base + NY * CAP + y * 2 + (slot >> 1), slot & 1


def routes(owner, slot):
    low_at, high_at, odd = targets(owner, slot)
    at = iota((ALL, TOK), 0)
    low = hot(at == low_at)
    even_hot = hot((at == high_at) & (odd == 0))
    odd_hot = hot((at == high_at) & (odd == 1))
    return low, even_hot, odd_hot


def pack(values, hots):
    low, even_hot, odd_hot = hots
    out = []
    for v in values:
        high = v[:, LOW:]
        none = jnp.zeros_like(high)
        out.append(
            dot(low, v[:, :LOW])
            + dot(even_hot, jnp.concatenate([high, none], axis=1))
            + dot(odd_hot, jnp.concatenate([none, high], axis=1))
        )
    return out


def unpack(rows, owner, slot):
    low_at, high_at, odd = (column(t).astype(I32) for t in targets(owner, slot))
    at = iota((TOK, ALL), 1)
    low = dot(hot(at == low_at), rows)
    even_rows = dot(hot((at == high_at) & (odd == 0)), rows)
    odd_rows = dot(hot((at == high_at) & (odd == 1)), rows)
    high = even_rows[:, : SHARE - LOW] + odd_rows[:, SHARE - LOW :]
    return jnp.concatenate([low, high], axis=1)


def row_of(ref, layer, core):
    return jnp.where(core == 0, ref[layer, 0:1, :], ref[layer, 1:2, :])


def joined(parts):
    parts = [p.reshape(NZ, ZROWS, LOW) for p in parts]
    return jnp.concatenate(parts, axis=1).reshape(len(parts) * ALL, LOW).astype(BF)


def start_kernel(core_ref, acts, cot, gates, owners, slots, out, tok, gate_v, owner_v, slot_v, sems):
    core = core_ref[0]
    copies = [
        pltpu.make_async_copy(src, dst, sems.at[k])
        for k, (src, dst) in enumerate(
            [
                (owners, owner_v),
                (slots, slot_v),
                (gates, gate_v),
                (cot.at[core], tok.at[0]),
                (acts.at[1, core], tok.at[1]),
            ]
        )
    ]
    for copy in copies:
        copy.start()
    copies[0].wait()
    copies[1].wait()
    upper = routes(row_of(owner_v, 1, core), row_of(slot_v, 1, core))
    for copy in copies[2:]:
        copy.wait()
    gate = column(row_of(gate_v, 1, core))
    scaled = (gate * tok[0].astype(F32)).astype(BF)
    first = pack([tok[1], scaled], upper)
    out[...] = joined(first)


def spread_move():
    shape = (NY, YROWS, ALL)
    y, k, at = iota(shape, 0), iota(shape, 1), iota(shape, 2)
    z = (k & 31) >> 1
    half = k & 1
    low = z * ZROWS + y * CAP + half * 2 + (k >> 5)
    high = z * ZROWS + NY * CAP + y * 2 + half
    return hot((at == jnp.where(k < NZ * CAP, low, high)).reshape(ALL, ALL))


def moved_parts(rows):
    move = spread_move()
    value = rows[...].astype(F32).reshape(NZ, 2 * ZROWS, LOW)
    for a in range(2):
        part = value[:, a * ZROWS : (a + 1) * ZROWS].reshape(ALL, LOW).astype(BF)
        yield a, dot(move, part).astype(BF)


def spread_kernel(rows, out):
    for a, moved in moved_parts(rows):
        for j in range(NY):
            for i in range(NX):
                out[j * NX + i, a * YROWS : (a + 1) * YROWS, :] = moved[j * YROWS : (j + 1) * YROWS]


def sending_kernel(rows, out, held_rows, sems):
    copies = []
    for a, moved in moved_parts(rows):
        held_rows[a] = moved.reshape(NY, YROWS, LOW)
        for i in range(NX):
            copy = pltpu.make_async_copy(held_rows.at[a], out.at[:, i, a * YROWS : (a + 1) * YROWS], sems.at[a, i])
            copy.start()
            copies.append(copy)
    for copy in copies:
        copy.wait()


def gather_kernel(parts, out):
    shape = (NZ, ZROWS, ALL)
    z, k, at = iota(shape, 0), iota(shape, 1), iota(shape, 2)
    low = (k >> 2) * YROWS + (k & 1) * 32 + z * 2 + ((k & 3) >> 1)
    k2 = k - NY * CAP
    high = (k2 >> 1) * YROWS + NZ * CAP + z * 2 + (k2 & 1)
    move = hot((at == jnp.where(k < NY * CAP, low, high)).reshape(ALL, ALL))
    sums = []
    for j in range(NY):
        total = parts[j * NX].astype(F32)
        for i in range(1, NX):
            total = total + parts[j * NX + i].astype(F32)
        sums.append(total)
    out[...] = dot(move, jnp.concatenate(sums, axis=0).astype(BF)).astype(BF)


def assemble(ref, first):
    rows = []
    for j in range(NY):
        cols = []
        for i in range(NX):
            low = ref[j * NX + i, first : first + 64, :]
            high = ref[j * NX + i, first + 64 : first + YROWS, :]
            cols.append(low)
            cols.append(jnp.concatenate([high[:, :64], high[:, 64:]], axis=0))
        rows.append(jnp.concatenate(cols, axis=1))
    return jnp.concatenate(rows, axis=0)


def expert_step(x, grad, w_in, w_out, out, save):
    save(3, grad)
    inv = lax.rsqrt(jnp.mean(x * x, axis=1, keepdims=True) + 1e-06)
    normed = (x * inv).astype(BF)
    save(0, normed)
    u = dot(normed, w_in())
    square = u * u
    s = jnp.tanh(0.7978845608 * (u + 0.044715 * square * u))
    save(2, (0.5 * u * (1.0 + s)).astype(BF))
    slope = 0.5 * (1.0 + s) + 0.5 * u * (1.0 - s * s) * 0.7978845608 * (1.0 + 0.134145 * square)
    back = (dot(grad, w_out(), 1, 1) * slope).astype(BF)
    save(1, back)
    part = dot(back, w_in(), 1, 1)
    inner = jnp.sum(part * x, axis=1, keepdims=True)
    branch = (inv * part - (inv * inv * inv * inner * (1.0 / WIDTH)) * x).astype(BF)
    for j in range(NY):
        for i in range(NX):
            at = i * SHARE
            block = branch[j * 64 : (j + 1) * 64]
            out[j * NX + i, 0:64, :] = block[:, at : at + LOW]
            out[j * NX + i, 64:YROWS, :] = jnp.concatenate(
                [block[:32, at + LOW : at + SHARE], block[32:, at + LOW : at + SHARE]], axis=1
            )


def held(ref):
    return lambda: ref[...]


def fetched(source, buffer, sems):
    step = WIDTH // CUTS
    copies = [
        pltpu.make_async_copy(source.at[k * step : (k + 1) * step], buffer.at[k * step : (k + 1) * step], sems.at[k])
        for k in range(CUTS)
    ]
    for copy in copies:
        copy.start()

    def value():
        while copies:
            copies.pop(0).wait()
        return buffer[...]

    return value


def upper_kernel(core_ref, saved, own_in, other_in, own_out, other_out, out, k0, k1, k2, k3, in_buf, out_buf, sems):
    def run(w_in, w_out):
        def save(k, value):
            (k0, k1, k2, k3)[k][...] = value

        expert_step(assemble(saved, 0).astype(F32), assemble(saved, YROWS), w_in, w_out, out, save)

    @pl.when(core_ref[0] == 1)
    def _():
        run(held(own_in), held(own_out))

    @pl.when(core_ref[0] != 1)
    def _():
        run(fetched(other_in, in_buf, sems.at[0]), fetched(other_out, out_buf, sems.at[1]))


def lower_kernel(
    core_ref, saved, n1, b1, h1, g1, own_in, other_in, own_out, other_out,
    out, k0, k1, k2, k3, give, kept, in_buf, out_buf, sems, more,
):
    keep, above = (k0, k1, k2, k3), (n1, b1, h1, g1)

    def run(w_in, w_out, save):
        expert_step(assemble(saved, 0).astype(F32), assemble(saved, YROWS), w_in, w_out, out, save)

    @pl.when(core_ref[0] == 0)
    def _():
        copies = [pltpu.make_async_copy(above[k], give.at[k], sems.at[k]) for k in range(4)]
        for copy in copies:
            copy.start()

        def save(k, value):
            keep[k][...] = value

        run(held(own_in), held(own_out), save)
        for copy in copies:
            copy.wait()

    @pl.when(core_ref[0] != 0)
    def _():
        w_in, w_out = fetched(other_in, in_buf, more.at[0]), fetched(other_out, out_buf, more.at[1])
        copies = [pltpu.make_async_copy(kept.at[k], give.at[k], sems.at[k]) for k in range(4)]

        def save(k, value):
            kept[k] = value
            copies[k].start()
            keep[k][...] = above[k][...]

        run(w_in, w_out, save)
        for copy in copies:
            copy.wait()


def weight_kernel(k0, k1, k2, k3, came, first, second, rows, sums, sems):
    half = NY * NZ * CAP
    loads = [
        [pltpu.make_async_copy(src, rows.at[k, n * half : (n + 1) * half], sems.at[2 * k + n])
         for n, src in enumerate([(k0, k1, k2, k3)[k], came.at[k]])]
        for k in range(4)
    ]
    for pair in loads:
        for copy in pair:
            copy.start()

    def product(k, at, dst):
        for copy in loads[k] + loads[k + 1]:
            copy.wait()
        sums[at] = dot(rows[k], rows[k + 1], 0, 0).astype(BF)
        copy = pltpu.make_async_copy(sums.at[at], dst, sems.at[8 + at])
        copy.start()
        return copy

    stores = [product(0, 0, first), product(2, 1, second)]
    for copy in stores:
        copy.wait()


def middle_kernel(core_ref, rows, cot, acts, gates, owners, slots, result, out):
    core = core_ref[0]
    branch = unpack(rows[...], row_of(owners, 1, core), row_of(slots, 1, core))
    res = (cot[core].astype(F32) + branch).astype(BF)
    result[...] = res
    gate = column(row_of(gates, 0, core))
    scaled = (gate * res.astype(F32)).astype(BF)
    out[...] = joined(pack([acts[0, core], scaled], routes(row_of(owners, 0, core), row_of(slots, 0, core))))


def end_kernel(core_ref, rows, above, owners, slots, grad_in, keep, give, same):
    core = core_ref[0]
    branch = unpack(rows[...], row_of(owners, 0, core), row_of(slots, 0, core))
    res = (above[...].astype(F32) + branch).astype(BF)
    keep[...] = jnp.where(core == 0, res, above[...])
    give[...] = jnp.where(core == 0, above[...], res)


VM = pl.BlockSpec(memory_space=pltpu.VMEM)
SM = pl.BlockSpec(memory_space=pltpu.SMEM)
HB = pl.BlockSpec(memory_space=pltpu.HBM)


def call(kernel, ins, outs, name, scratch=(), mib=16, cost=None, places=None, alias=None):
    return pl.pallas_call(
        kernel,
        in_specs=list(ins),
        out_specs=places or [VM] * len(outs),
        out_shape=[o if hasattr(o, "dtype") else jax.ShapeDtypeStruct(o, BF) for o in outs],
        scratch_shapes=list(scratch),
        compiler_params=pltpu.CompilerParams(vmem_limit_bytes=mib << 20),
        cost_estimate=cost and pl.CostEstimate(flops=cost[0], bytes_accessed=cost[1], transcendentals=0),
        input_output_aliases=alias or {},
        name=name,
    )


def over_z(x):
    ring = [[(FIRST + k) % NZ for k in range(NZ)]]
    x = x.reshape(NZ, -1, LOW)
    return lax.all_to_all(x, "z", 0, 0, axis_index_groups=ring, tiled=True).reshape(-1, LOW)


def over_yx(x):
    return lax.all_to_all(x, ("y", "pair"), 0, 0, tiled=True)


def body(acts, cotangent, gates, owners, slots, w_in, w_out):
    index = lax.axis_index("segment")
    top = index == 1
    core = index.astype(I32).reshape(1)
    own_in, own_out = w_in[0, 0], w_out[0, 0]
    other_in = lax.ppermute(own_in, "segment", SWAP)
    other_out = lax.ppermute(own_out, "segment", SWAP)
    weights = (own_in, other_in, own_out, other_out)

    table = (2, 2, TOK)
    (packed,) = call(
        start_kernel, [SM] + [HB] * 5, [(2 * ALL, LOW)], "start",
        [pltpu.VMEM((2, TOK, SHARE), BF), pltpu.VMEM(table, F32), pltpu.VMEM(table, I32),
         pltpu.VMEM(table, I32), pltpu.SemaphoreType.DMA((6,))], mib=60,
    )(core, acts, cotangent, gates, owners, slots)
    (sent,) = call(
        sending_kernel, [VM], [(NY, NX, 2 * YROWS, LOW)], "sending",
        [pltpu.VMEM((2, NY, YROWS, LOW), BF), pltpu.SemaphoreType.DMA((2, NX))], places=[HB], mib=61,
    )(over_z(packed))
    saved = over_yx(sent.reshape(NY * NX, 2 * YROWS, LOW))
    blocks, wide = (NY * NX, YROWS, LOW), (NY * NZ * CAP, WIDTH)
    parts, *kept1 = call(
        upper_kernel, [SM, VM] + [VM, HB] * 2, [blocks] + [wide] * 4, "upper",
        [pltpu.VMEM((WIDTH, HID), BF), pltpu.VMEM((HID, WIDTH), BF), pltpu.SemaphoreType.DMA((2, CUTS))],
    )(core, saved, *weights)
    (rows,) = call(gather_kernel, [VM], [(ALL, LOW)], "gather")(over_yx(parts))
    res1, packed = call(middle_kernel, [SM] + [VM] * 6, [(TOK, SHARE), (2 * ALL, LOW)], "middle")(
        core, over_z(rows), cotangent, acts, gates, owners, slots
    )
    (sent,) = call(spread_kernel, [VM], [(NY * NX, 2 * YROWS, LOW)], "spread")(
        over_z(packed)
    )
    parts, *keep, give = call(
        lower_kernel, [SM] + [VM] * 5 + [VM, HB] * 2, [blocks] + [wide] * 4 + [(4,) + wide], "lower",
        [pltpu.VMEM((4,) + wide, BF), pltpu.VMEM((WIDTH, HID), BF), pltpu.VMEM((HID, WIDTH), BF),
         pltpu.SemaphoreType.DMA((4,)), pltpu.SemaphoreType.DMA((2, CUTS))], places=[VM] * 5 + [HB],
    )(core, over_yx(sent), *kept1, *weights)
    came = lax.ppermute(give, "segment", SWAP)
    (rows,) = call(gather_kernel, [VM], [(ALL, LOW)], "gather")(over_yx(parts))

    grad_in, grad_out = call(
        weight_kernel, [HB] * 5, [(WIDTH, HID), (HID, WIDTH)], "weight",
        [pltpu.VMEM((4, 2 * NY * NZ * CAP, WIDTH), BF), pltpu.VMEM((2, WIDTH, HID), BF), pltpu.SemaphoreType.DMA((10,))],
        mib=56, cost=(2 * 10**9, 6 * 10**6), places=[HB, HB],
    )(*keep, came)
    mine, other, grad_in = call(
        end_kernel, [SM] + [VM] * 4 + [HB], [(TOK, SHARE)] * 2 + [(WIDTH, HID)], "end",
        places=[VM, VM, HB], alias={5: 2},
    )(core, over_z(rows), res1, owners, slots, grad_in)
    got = lax.ppermute(other, "segment", SWAP)
    grads = jnp.stack([jnp.where(top, got, mine), jnp.where(top, mine, got)])
    return grads[None], grad_in[None, None], grad_out[None, None]


def solution(mesh):
    fine = Mesh(mesh.devices.reshape(2, NY, NZ, NX), ("segment", "y", "z", "pair"))
    e = ("y", "z")
    placed = (
        P(None, None, e, "pair"),
        P(None, e, "pair"),
        P(None, None, e),
        P(None, None, e),
        P(None, None, e),
        P("segment", e, None, "pair"),
        P("segment", e, "pair", None),
    )
    return jax.shard_map(
        body,
        mesh=fine,
        in_specs=placed,
        out_specs=(
            P("segment", None, e, "pair"),
            P("segment", e, None, "pair"),
            P("segment", e, "pair", None),
        ),
        check_vma=False,
    )
```

```python
import functools

import jax
import jax.numpy as jnp
from jax import lax
from jax.experimental import pallas as pl
from jax.experimental.pallas import tpu as pltpu
from jax.sharding import Mesh, PartitionSpec as P

BF = jnp.bfloat16
F32 = jnp.float32
I32 = jnp.int32
SWAP = [(0, 1), (1, 0)]

NY, NZ, NX = 4, 16, 4
CAP = 4
TOK = 192
SHARE = 192
WIDTH = SHARE * NX
FIRST = NZ // 2
HID = 768
LOW = 128
ZROWS = NY * CAP + NY * CAP // 2
YROWS = NZ * CAP + NZ * CAP // 2
CUTS = 4
ALL = NZ * ZROWS


def dot(a, b, ca=1, cb=0):
    return lax.dot_general(a, b, (((ca,), (cb,)), ((), ())), preferred_element_type=F32)


def hot(cond):
    return jnp.where(cond, 1.0, 0.0).astype(BF)


def iota(shape, dim):
    return lax.broadcasted_iota(I32, shape, dim)


def column(row):
    n = row.shape[1]
    eye = iota((n, n), 0) == iota((n, n), 1)
    return jnp.sum(jnp.where(eye, row.astype(F32), 0.0), axis=1, keepdims=True)


def targets(owner, slot):
    base = ((owner + FIRST) & (NZ - 1)) * ZROWS
    y = owner >> 4
    return base + y * CAP + slot, base + NY * CAP + y * 2 + (slot >> 1), slot & 1


def routes(owner, slot):
    low_at, high_at, odd = targets(owner, slot)
    at = iota((ALL, TOK), 0)
    low = hot(at == low_at)
    even_hot = hot((at == high_at) & (odd == 0))
    odd_hot = hot((at == high_at) & (odd == 1))
    return low, even_hot, odd_hot


def pack(values, hots):
    low, even_hot, odd_hot = hots
    out = []
    for v in values:
        high = v[:, LOW:]
        none = jnp.zeros_like(high)
        out.append(
            dot(low, v[:, :LOW])
            + dot(even_hot, jnp.concatenate([high, none], axis=1))
            + dot(odd_hot, jnp.concatenate([none, high], axis=1))
        )
    return out


def unpack(rows, owner, slot):
    low_at, high_at, odd = (column(t).astype(I32) for t in targets(owner, slot))
    at = iota((TOK, ALL), 1)
    low = dot(hot(at == low_at), rows)
    even_rows = dot(hot((at == high_at) & (odd == 0)), rows)
    odd_rows = dot(hot((at == high_at) & (odd == 1)), rows)
    high = even_rows[:, : SHARE - LOW] + odd_rows[:, SHARE - LOW :]
    return jnp.concatenate([low, high], axis=1)


def row_of(ref, layer, core):
    return jnp.where(core == 0, ref[layer, 0:1, :], ref[layer, 1:2, :])


def joined(parts):
    parts = [p.reshape(NZ, ZROWS, LOW) for p in parts]
    return jnp.concatenate(parts, axis=1).reshape(len(parts) * ALL, LOW).astype(BF)


def start_kernel(core_ref, acts, cot, gates, owners, slots, out, tok, gate_v, owner_v, slot_v, sems):
    core = core_ref[0]
    copies = [
        pltpu.make_async_copy(src, dst, sems.at[k])
        for k, (src, dst) in enumerate(
            [
                (owners, owner_v),
                (slots, slot_v),
                (gates, gate_v),
                (cot.at[core], tok.at[0]),
                (acts.at[1, core], tok.at[1]),
            ]
        )
    ]
    for copy in copies:
        copy.start()
    copies[0].wait()
    copies[1].wait()
    upper = routes(row_of(owner_v, 1, core), row_of(slot_v, 1, core))
    for copy in copies[2:]:
        copy.wait()
    gate = column(row_of(gate_v, 1, core))
    scaled = (gate * tok[0].astype(F32)).astype(BF)
    first = pack([tok[1], scaled], upper)
    out[...] = joined(first)


def spread_move():
    shape = (NY, YROWS, ALL)
    y, k, at = iota(shape, 0), iota(shape, 1), iota(shape, 2)
    z = (k & 31) >> 1
    half = k & 1
    low = z * ZROWS + y * CAP + half * 2 + (k >> 5)
    high = z * ZROWS + NY * CAP + y * 2 + half
    return hot((at == jnp.where(k < NZ * CAP, low, high)).reshape(ALL, ALL))


def moved_parts(rows):
    move = spread_move()
    value = rows[...].astype(F32).reshape(NZ, 2 * ZROWS, LOW)
    for a in range(2):
        part = value[:, a * ZROWS : (a + 1) * ZROWS].reshape(ALL, LOW).astype(BF)
        yield a, dot(move, part).astype(BF)


def spread_kernel(rows, out):
    for a, moved in moved_parts(rows):
        for j in range(NY):
            for i in range(NX):
                out[j * NX + i, a * YROWS : (a + 1) * YROWS, :] = moved[j * YROWS : (j + 1) * YROWS]


def spread_after_kernel(rows, one, two, out):
    spread_kernel(rows, out)


def gather_kernel(parts, out):
    shape = (NZ, ZROWS, ALL)
    z, k, at = iota(shape, 0), iota(shape, 1), iota(shape, 2)
    low = (k >> 2) * YROWS + (k & 1) * 32 + z * 2 + ((k & 3) >> 1)
    k2 = k - NY * CAP
    high = (k2 >> 1) * YROWS + NZ * CAP + z * 2 + (k2 & 1)
    move = hot((at == jnp.where(k < NY * CAP, low, high)).reshape(ALL, ALL))
    sums = []
    for j in range(NY):
        total = parts[j * NX].astype(F32)
        for i in range(1, NX):
            total = total + parts[j * NX + i].astype(F32)
        sums.append(total)
    out[...] = dot(move, jnp.concatenate(sums, axis=0).astype(BF)).astype(BF)


def assemble(ref, first):
    rows = []
    for j in range(NY):
        cols = []
        for i in range(NX):
            low = ref[j * NX + i, first : first + 64, :]
            high = ref[j * NX + i, first + 64 : first + YROWS, :]
            cols.append(low)
            cols.append(jnp.concatenate([high[:, :64], high[:, 64:]], axis=0))
        rows.append(jnp.concatenate(cols, axis=1))
    return jnp.concatenate(rows, axis=0)


def expert_step(x, grad, w_in, w_out, out, save):
    save(3, grad)
    inv = lax.rsqrt(jnp.mean(x * x, axis=1, keepdims=True) + 1e-06)
    normed = (x * inv).astype(BF)
    save(0, normed)
    u = dot(normed, w_in())
    square = u * u
    s = jnp.tanh(0.7978845608 * (u + 0.044715 * square * u))
    save(2, (0.5 * u * (1.0 + s)).astype(BF))
    slope = 0.5 * (1.0 + s) + 0.5 * u * (1.0 - s * s) * 0.7978845608 * (1.0 + 0.134145 * square)
    back = (dot(grad, w_out(), 1, 1) * slope).astype(BF)
    save(1, back)
    part = dot(back, w_in(), 1, 1)
    inner = jnp.sum(part * x, axis=1, keepdims=True)
    branch = (inv * part - (inv * inv * inv * inner * (1.0 / WIDTH)) * x).astype(BF)
    for j in range(NY):
        for i in range(NX):
            at = i * SHARE
            block = branch[j * 64 : (j + 1) * 64]
            out[j * NX + i, 0:64, :] = block[:, at : at + LOW]
            out[j * NX + i, 64:YROWS, :] = jnp.concatenate(
                [block[:32, at + LOW : at + SHARE], block[32:, at + LOW : at + SHARE]], axis=1
            )


def held(ref):
    return lambda: ref[...]


def fetched(source, buffer, sems):
    step = WIDTH // CUTS
    copies = [
        pltpu.make_async_copy(source.at[k * step : (k + 1) * step], buffer.at[k * step : (k + 1) * step], sems.at[k])
        for k in range(CUTS)
    ]
    for copy in copies:
        copy.start()

    def value():
        while copies:
            copies.pop(0).wait()
        return buffer[...]

    return value


def upper_kernel(core_ref, saved, own_in, other_in, own_out, other_out, out, k0, k1, k2, k3, in_buf, out_buf, sems):
    def run(w_in, w_out):
        def save(k, value):
            (k0, k1, k2, k3)[k][...] = value

        expert_step(assemble(saved, 0).astype(F32), assemble(saved, YROWS), w_in, w_out, out, save)

    @pl.when(core_ref[0] == 1)
    def _():
        run(held(own_in), held(own_out))

    @pl.when(core_ref[0] != 1)
    def _():
        run(fetched(other_in, in_buf, sems.at[0]), fetched(other_out, out_buf, sems.at[1]))


def lower_kernel(
    core_ref, saved, n1, b1, h1, g1, own_in, other_in, own_out, other_out,
    out, k0, k1, k2, k3, give, kept, in_buf, out_buf, sems, more,
):
    keep, above = (k0, k1, k2, k3), (n1, b1, h1, g1)

    def run(w_in, w_out, save):
        expert_step(assemble(saved, 0).astype(F32), assemble(saved, YROWS), w_in, w_out, out, save)

    @pl.when(core_ref[0] == 0)
    def _():
        copies = [pltpu.make_async_copy(above[k], give.at[k], sems.at[k]) for k in range(4)]
        for copy in copies:
            copy.start()

        def save(k, value):
            keep[k][...] = value

        run(held(own_in), held(own_out), save)
        for copy in copies:
            copy.wait()

    @pl.when(core_ref[0] != 0)
    def _():
        w_in, w_out = fetched(other_in, in_buf, more.at[0]), fetched(other_out, out_buf, more.at[1])
        copies = [pltpu.make_async_copy(kept.at[k], give.at[k], sems.at[k]) for k in range(4)]

        def save(k, value):
            kept[k] = value
            copies[k].start()
            keep[k][...] = above[k][...]

        run(w_in, w_out, save)
        for copy in copies:
            copy.wait()


def weight_kernel(k0, k1, k2, k3, came, first, second, rows, sums, sems):
    half = NY * NZ * CAP
    loads = [
        [pltpu.make_async_copy(src, rows.at[k, n * half : (n + 1) * half], sems.at[2 * k + n])
         for n, src in enumerate([(k0, k1, k2, k3)[k], came.at[k]])]
        for k in range(4)
    ]
    for pair in loads:
        for copy in pair:
            copy.start()

    def product(k, at, dst):
        for copy in loads[k] + loads[k + 1]:
            copy.wait()
        sums[at] = dot(rows[k], rows[k + 1], 0, 0).astype(BF)
        copy = pltpu.make_async_copy(sums.at[at], dst, sems.at[8 + at])
        copy.start()
        return copy

    stores = [product(0, 0, first), product(2, 1, second)]
    for copy in stores:
        copy.wait()


def middle_kernel(core_ref, rows, cot, acts, gates, owners, slots, result, out):
    core = core_ref[0]
    branch = unpack(rows[...], row_of(owners, 1, core), row_of(slots, 1, core))
    res = (cot[core].astype(F32) + branch).astype(BF)
    result[...] = res
    gate = column(row_of(gates, 0, core))
    scaled = (gate * res.astype(F32)).astype(BF)
    out[...] = joined(pack([acts[0, core], scaled], routes(row_of(owners, 0, core), row_of(slots, 0, core))))


def end_kernel(core_ref, rows, above, owners, slots, grad_in, keep, give, same):
    core = core_ref[0]
    branch = unpack(rows[...], row_of(owners, 0, core), row_of(slots, 0, core))
    res = (above[...].astype(F32) + branch).astype(BF)
    keep[...] = jnp.where(core == 0, res, above[...])
    give[...] = jnp.where(core == 0, above[...], res)


VM = pl.BlockSpec(memory_space=pltpu.VMEM)
SM = pl.BlockSpec(memory_space=pltpu.SMEM)
HB = pl.BlockSpec(memory_space=pltpu.HBM)


def call(kernel, ins, outs, name, scratch=(), mib=16, cost=None, places=None, alias=None):
    return pl.pallas_call(
        kernel,
        in_specs=list(ins),
        out_specs=places or [VM] * len(outs),
        out_shape=[o if hasattr(o, "dtype") else jax.ShapeDtypeStruct(o, BF) for o in outs],
        scratch_shapes=list(scratch),
        compiler_params=pltpu.CompilerParams(vmem_limit_bytes=mib << 20),
        cost_estimate=cost and pl.CostEstimate(flops=cost[0], bytes_accessed=cost[1], transcendentals=0),
        input_output_aliases=alias or {},
        name=name,
    )


def over_z(x):
    ring = [[(FIRST + k) % NZ for k in range(NZ)]]
    x = x.reshape(NZ, -1, LOW)
    return lax.all_to_all(x, "z", 0, 0, axis_index_groups=ring, tiled=True).reshape(-1, LOW)


def over_yx(x):
    return lax.all_to_all(x, ("y", "pair"), 0, 0, tiled=True)


def body(acts, cotangent, gates, owners, slots, w_in, w_out):
    index = lax.axis_index("segment")
    top = index == 1
    core = index.astype(I32).reshape(1)
    own_in, own_out = w_in[0, 0], w_out[0, 0]
    other_in = lax.ppermute(own_in, "segment", SWAP)
    other_out = lax.ppermute(own_out, "segment", SWAP)
    weights = (own_in, other_in, own_out, other_out)

    table = (2, 2, TOK)
    (packed,) = call(
        start_kernel, [SM] + [HB] * 5, [(2 * ALL, LOW)], "start",
        [pltpu.VMEM((2, TOK, SHARE), BF), pltpu.VMEM(table, F32), pltpu.VMEM(table, I32),
         pltpu.VMEM(table, I32), pltpu.SemaphoreType.DMA((6,))], mib=60,
    )(core, acts, cotangent, gates, owners, slots)
    (sent,) = call(spread_after_kernel, [VM, HB, HB], [(NY * NX, 2 * YROWS, LOW)], "spread_after")(
        over_z(packed), other_in, other_out
    )
    saved = over_yx(sent)
    blocks, wide = (NY * NX, YROWS, LOW), (NY * NZ * CAP, WIDTH)
    parts, *kept1 = call(
        upper_kernel, [SM, VM] + [VM, HB] * 2, [blocks] + [wide] * 4, "upper",
        [pltpu.VMEM((WIDTH, HID), BF), pltpu.VMEM((HID, WIDTH), BF), pltpu.SemaphoreType.DMA((2, CUTS))],
    )(core, saved, *weights)
    (rows,) = call(gather_kernel, [VM], [(ALL, LOW)], "gather")(over_yx(parts))
    res1, packed = call(middle_kernel, [SM] + [VM] * 6, [(TOK, SHARE), (2 * ALL, LOW)], "middle")(
        core, over_z(rows), cotangent, acts, gates, owners, slots
    )
    (sent,) = call(spread_kernel, [VM], [(NY * NX, 2 * YROWS, LOW)], "spread")(
        over_z(packed)
    )
    parts, *keep, give = call(
        lower_kernel, [SM] + [VM] * 5 + [VM, HB] * 2, [blocks] + [wide] * 4 + [(4,) + wide], "lower",
        [pltpu.VMEM((4,) + wide, BF), pltpu.VMEM((WIDTH, HID), BF), pltpu.VMEM((HID, WIDTH), BF),
         pltpu.SemaphoreType.DMA((4,)), pltpu.SemaphoreType.DMA((2, CUTS))], places=[VM] * 5 + [HB],
    )(core, over_yx(sent), *kept1, *weights)
    came = lax.ppermute(give, "segment", SWAP)
    (rows,) = call(gather_kernel, [VM], [(ALL, LOW)], "gather")(over_yx(parts))

    grad_in, grad_out = call(
        weight_kernel, [HB] * 5, [(WIDTH, HID), (HID, WIDTH)], "weight",
        [pltpu.VMEM((4, 2 * NY * NZ * CAP, WIDTH), BF), pltpu.VMEM((2, WIDTH, HID), BF), pltpu.SemaphoreType.DMA((10,))],
        mib=56, cost=(2 * 10**9, 6 * 10**6), places=[HB, HB],
    )(*keep, came)
    mine, other, grad_in = call(
        end_kernel, [SM] + [VM] * 4 + [HB], [(TOK, SHARE)] * 2 + [(WIDTH, HID)], "end",
        places=[VM, VM, HB], alias={5: 2},
    )(core, over_z(rows), res1, owners, slots, grad_in)
    got = lax.ppermute(other, "segment", SWAP)
    grads = jnp.stack([jnp.where(top, got, mine), jnp.where(top, mine, got)])
    return grads[None], grad_in[None, None], grad_out[None, None]


def solution(mesh):
    fine = Mesh(mesh.devices.reshape(2, NY, NZ, NX), ("segment", "y", "z", "pair"))
    e = ("y", "z")
    placed = (
        P(None, None, e, "pair"),
        P(None, e, "pair"),
        P(None, None, e),
        P(None, None, e),
        P(None, None, e),
        P("segment", e, None, "pair"),
        P("segment", e, "pair", None),
    )
    return jax.shard_map(
        body,
        mesh=fine,
        in_specs=placed,
        out_specs=(
            P("segment", None, e, "pair"),
            P("segment", e, None, "pair"),
            P("segment", e, "pair", None),
        ),
        check_vma=False,
    )
```

```python
import functools

import jax
import jax.numpy as jnp
from jax import lax
from jax.experimental import pallas as pl
from jax.experimental.pallas import tpu as pltpu
from jax.sharding import Mesh, PartitionSpec as P

BF = jnp.bfloat16
F32 = jnp.float32
I32 = jnp.int32
SWAP = [(0, 1), (1, 0)]

NY, NZ, NX = 4, 16, 4
CAP = 4
TOK = 192
SHARE = 192
WIDTH = SHARE * NX
FIRST = NZ // 2
HID = 768
LOW = 128
ZROWS = NY * CAP + NY * CAP // 2
YROWS = NZ * CAP + NZ * CAP // 2
CUTS = 4
ALL = NZ * ZROWS


def dot(a, b, ca=1, cb=0):
    return lax.dot_general(a, b, (((ca,), (cb,)), ((), ())), preferred_element_type=F32)


def hot(cond):
    return jnp.where(cond, 1.0, 0.0).astype(BF)


def iota(shape, dim):
    return lax.broadcasted_iota(I32, shape, dim)


def column(row):
    n = row.shape[1]
    eye = iota((n, n), 0) == iota((n, n), 1)
    return jnp.sum(jnp.where(eye, row.astype(F32), 0.0), axis=1, keepdims=True)


def targets(owner, slot):
    base = ((owner + FIRST) & (NZ - 1)) * ZROWS
    y = owner >> 4
    return base + y * CAP + slot, base + NY * CAP + y * 2 + (slot >> 1), slot & 1


def routes(owner, slot):
    low_at, high_at, odd = targets(owner, slot)
    at = iota((ALL, TOK), 0)
    low = hot(at == low_at)
    even_hot = hot((at == high_at) & (odd == 0))
    odd_hot = hot((at == high_at) & (odd == 1))
    return low, even_hot, odd_hot


def pack(values, hots):
    low, even_hot, odd_hot = hots
    out = []
    for v in values:
        high = v[:, LOW:]
        none = jnp.zeros_like(high)
        out.append(
            dot(low, v[:, :LOW])
            + dot(even_hot, jnp.concatenate([high, none], axis=1))
            + dot(odd_hot, jnp.concatenate([none, high], axis=1))
        )
    return out


def unpack(rows, owner, slot):
    low_at, high_at, odd = (column(t).astype(I32) for t in targets(owner, slot))
    at = iota((TOK, ALL), 1)
    low = dot(hot(at == low_at), rows)
    even_rows = dot(hot((at == high_at) & (odd == 0)), rows)
    odd_rows = dot(hot((at == high_at) & (odd == 1)), rows)
    high = even_rows[:, : SHARE - LOW] + odd_rows[:, SHARE - LOW :]
    return jnp.concatenate([low, high], axis=1)


def row_of(ref, layer, core):
    return jnp.where(core == 0, ref[layer, 0:1, :], ref[layer, 1:2, :])


def joined(parts):
    parts = [p.reshape(NZ, ZROWS, LOW) for p in parts]
    return jnp.concatenate(parts, axis=1).reshape(len(parts) * ALL, LOW).astype(BF)


def start_kernel(core_ref, acts, cot, gates, owners, slots, out, tok, gate_v, owner_v, slot_v, sems):
    core = core_ref[0]
    copies = [
        pltpu.make_async_copy(src, dst, sems.at[k])
        for k, (src, dst) in enumerate(
            [
                (owners, owner_v),
                (slots, slot_v),
                (gates, gate_v),
                (cot.at[core], tok.at[0]),
                (acts.at[1, core], tok.at[1]),
            ]
        )
    ]
    for copy in copies:
        copy.start()
    copies[0].wait()
    copies[1].wait()
    upper = routes(row_of(owner_v, 1, core), row_of(slot_v, 1, core))
    for copy in copies[2:]:
        copy.wait()
    gate = column(row_of(gate_v, 1, core))
    scaled = (gate * tok[0].astype(F32)).astype(BF)
    first = pack([tok[1], scaled], upper)
    out[...] = joined(first)


def spread_move():
    shape = (NY, YROWS, ALL)
    y, k, at = iota(shape, 0), iota(shape, 1), iota(shape, 2)
    z = (k & 31) >> 1
    half = k & 1
    low = z * ZROWS + y * CAP + half * 2 + (k >> 5)
    high = z * ZROWS + NY * CAP + y * 2 + half
    return hot((at == jnp.where(k < NZ * CAP, low, high)).reshape(ALL, ALL))


def moved_parts(rows):
    move = spread_move()
    value = rows[...].astype(F32).reshape(NZ, 2 * ZROWS, LOW)
    for a in range(2):
        part = value[:, a * ZROWS : (a + 1) * ZROWS].reshape(ALL, LOW).astype(BF)
        yield a, dot(move, part).astype(BF)


def spread_kernel(rows, out):
    for a, moved in moved_parts(rows):
        for j in range(NY):
            for i in range(NX):
                out[j * NX + i, a * YROWS : (a + 1) * YROWS, :] = moved[j * YROWS : (j + 1) * YROWS]


def gather_kernel(parts, out):
    shape = (NZ, ZROWS, ALL)
    z, k, at = iota(shape, 0), iota(shape, 1), iota(shape, 2)
    low = (k >> 2) * YROWS + (k & 1) * 32 + z * 2 + ((k & 3) >> 1)
    k2 = k - NY * CAP
    high = (k2 >> 1) * YROWS + NZ * CAP + z * 2 + (k2 & 1)
    move = hot((at == jnp.where(k < NY * CAP, low, high)).reshape(ALL, ALL))
    sums = []
    for j in range(NY):
        total = parts[j * NX].astype(F32)
        for i in range(1, NX):
            total = total + parts[j * NX + i].astype(F32)
        sums.append(total)
    out[...] = dot(move, jnp.concatenate(sums, axis=0).astype(BF)).astype(BF)


def assemble(ref, first):
    rows = []
    for j in range(NY):
        cols = []
        for i in range(NX):
            low = ref[j * NX + i, first : first + 64, :]
            high = ref[j * NX + i, first + 64 : first + YROWS, :]
            cols.append(low)
            cols.append(jnp.concatenate([high[:, :64], high[:, 64:]], axis=0))
        rows.append(jnp.concatenate(cols, axis=1))
    return jnp.concatenate(rows, axis=0)


def expert_step(x, grad, w_in, w_out, out, save):
    save(3, grad)
    inv = lax.rsqrt(jnp.mean(x * x, axis=1, keepdims=True) + 1e-06)
    normed = (x * inv).astype(BF)
    save(0, normed)
    u = dot(normed, w_in())
    square = u * u
    s = jnp.tanh(0.7978845608 * (u + 0.044715 * square * u))
    save(2, (0.5 * u * (1.0 + s)).astype(BF))
    slope = 0.5 * (1.0 + s) + 0.5 * u * (1.0 - s * s) * 0.7978845608 * (1.0 + 0.134145 * square)
    back = (dot(grad, w_out(), 1, 1) * slope).astype(BF)
    save(1, back)
    part = dot(back, w_in(), 1, 1)
    inner = jnp.sum(part * x, axis=1, keepdims=True)
    branch = (inv * part - (inv * inv * inv * inner * (1.0 / WIDTH)) * x).astype(BF)
    for j in range(NY):
        for i in range(NX):
            at = i * SHARE
            block = branch[j * 64 : (j + 1) * 64]
            out[j * NX + i, 0:64, :] = block[:, at : at + LOW]
            out[j * NX + i, 64:YROWS, :] = jnp.concatenate(
                [block[:32, at + LOW : at + SHARE], block[32:, at + LOW : at + SHARE]], axis=1
            )


def held(ref):
    return lambda: ref[...]


def fetched(source, buffer, sems):
    step = WIDTH // CUTS
    copies = [
        pltpu.make_async_copy(source.at[k * step : (k + 1) * step], buffer.at[k * step : (k + 1) * step], sems.at[k])
        for k in range(CUTS)
    ]
    for copy in copies:
        copy.start()

    def value():
        while copies:
            copies.pop(0).wait()
        return buffer[...]

    return value


def upper_kernel(core_ref, saved, own_in, other_in, own_out, other_out, out, k0, k1, k2, k3, in_buf, out_buf, sems):
    def run(w_in, w_out):
        def save(k, value):
            (k0, k1, k2, k3)[k][...] = value

        expert_step(assemble(saved, 0).astype(F32), assemble(saved, YROWS), w_in, w_out, out, save)

    @pl.when(core_ref[0] == 1)
    def _():
        run(held(own_in), held(own_out))

    @pl.when(core_ref[0] != 1)
    def _():
        run(fetched(other_in, in_buf, sems.at[0]), fetched(other_out, out_buf, sems.at[1]))


def lower_kernel(
    core_ref, saved, n1, b1, h1, g1, own_in, other_in, own_out, other_out,
    out, k0, k1, k2, k3, give, kept, in_buf, out_buf, sems, more,
):
    keep, above = (k0, k1, k2, k3), (n1, b1, h1, g1)

    def run(w_in, w_out, save):
        expert_step(assemble(saved, 0).astype(F32), assemble(saved, YROWS), w_in, w_out, out, save)

    @pl.when(core_ref[0] == 0)
    def _():
        copies = [pltpu.make_async_copy(above[k], give.at[k], sems.at[k]) for k in range(4)]
        for copy in copies:
            copy.start()

        def save(k, value):
            keep[k][...] = value

        run(held(own_in), held(own_out), save)
        for copy in copies:
            copy.wait()

    @pl.when(core_ref[0] != 0)
    def _():
        w_in, w_out = fetched(other_in, in_buf, more.at[0]), fetched(other_out, out_buf, more.at[1])
        copies = [pltpu.make_async_copy(kept.at[k], give.at[k], sems.at[k]) for k in range(4)]

        def save(k, value):
            kept[k] = value
            copies[k].start()
            keep[k][...] = above[k][...]

        run(w_in, w_out, save)
        for copy in copies:
            copy.wait()


def weight_kernel(k0, k1, k2, k3, came, first, second, rows, sums, sems):
    half = NY * NZ * CAP
    loads = [
        [pltpu.make_async_copy(src, rows.at[k, n * half : (n + 1) * half], sems.at[2 * k + n])
         for n, src in enumerate([(k0, k1, k2, k3)[k], came.at[k]])]
        for k in range(4)
    ]
    for pair in loads:
        for copy in pair:
            copy.start()

    def product(k, at, dst):
        for copy in loads[k] + loads[k + 1]:
            copy.wait()
        sums[at] = dot(rows[k], rows[k + 1], 0, 0).astype(BF)
        copy = pltpu.make_async_copy(sums.at[at], dst, sems.at[8 + at])
        copy.start()
        return copy

    stores = [product(0, 0, first), product(2, 1, second)]
    for copy in stores:
        copy.wait()


def middle_kernel(core_ref, rows, cot, acts, gates, owners, slots, result, out):
    core = core_ref[0]
    branch = unpack(rows[...], row_of(owners, 1, core), row_of(slots, 1, core))
    res = (cot[core].astype(F32) + branch).astype(BF)
    result[...] = res
    gate = column(row_of(gates, 0, core))
    scaled = (gate * res.astype(F32)).astype(BF)
    out[...] = joined(pack([acts[0, core], scaled], routes(row_of(owners, 0, core), row_of(slots, 0, core))))


def end_kernel(core_ref, rows, above, owners, slots, grad_in, keep, give, same):
    core = core_ref[0]
    branch = unpack(rows[...], row_of(owners, 0, core), row_of(slots, 0, core))
    res = (above[...].astype(F32) + branch).astype(BF)
    keep[...] = jnp.where(core == 0, res, above[...])
    give[...] = jnp.where(core == 0, above[...], res)


VM = pl.BlockSpec(memory_space=pltpu.VMEM)
SM = pl.BlockSpec(memory_space=pltpu.SMEM)
HB = pl.BlockSpec(memory_space=pltpu.HBM)


def call(kernel, ins, outs, name, scratch=(), mib=16, cost=None, places=None, alias=None):
    return pl.pallas_call(
        kernel,
        in_specs=list(ins),
        out_specs=places or [VM] * len(outs),
        out_shape=[o if hasattr(o, "dtype") else jax.ShapeDtypeStruct(o, BF) for o in outs],
        scratch_shapes=list(scratch),
        compiler_params=pltpu.CompilerParams(vmem_limit_bytes=mib << 20),
        cost_estimate=cost and pl.CostEstimate(flops=cost[0], bytes_accessed=cost[1], transcendentals=0),
        input_output_aliases=alias or {},
        name=name,
    )


def over_z(x):
    ring = [[(FIRST + k) % NZ for k in range(NZ)]]
    x = x.reshape(NZ, -1, LOW)
    return lax.all_to_all(x, "z", 0, 0, axis_index_groups=ring, tiled=True).reshape(-1, LOW)


def over_yx(x):
    return lax.all_to_all(x, ("y", "pair"), 0, 0, tiled=True)


def body(acts, cotangent, gates, owners, slots, w_in, w_out):
    index = lax.axis_index("segment")
    top = index == 1
    core = index.astype(I32).reshape(1)
    own_in, own_out = w_in[0, 0], w_out[0, 0]
    other_in = lax.ppermute(own_in, "segment", SWAP)
    other_out = lax.ppermute(own_out, "segment", SWAP)
    weights = (own_in, other_in, own_out, other_out)

    table = (2, 2, TOK)
    (packed,) = call(
        start_kernel, [SM] + [HB] * 5, [(2 * ALL, LOW)], "start",
        [pltpu.VMEM((2, TOK, SHARE), BF), pltpu.VMEM(table, F32), pltpu.VMEM(table, I32),
         pltpu.VMEM(table, I32), pltpu.SemaphoreType.DMA((6,))], mib=60,
    )(core, acts, cotangent, gates, owners, slots)
    (sent,) = call(spread_kernel, [VM], [(NY * NX, 2 * YROWS, LOW)], "spread", mib=60)(
        over_z(packed)
    )
    saved = over_yx(sent)
    blocks, wide = (NY * NX, YROWS, LOW), (NY * NZ * CAP, WIDTH)
    parts, *kept1 = call(
        upper_kernel, [SM, VM] + [VM, HB] * 2, [blocks] + [wide] * 4, "upper",
        [pltpu.VMEM((WIDTH, HID), BF), pltpu.VMEM((HID, WIDTH), BF), pltpu.SemaphoreType.DMA((2, CUTS))],
    )(core, saved, *weights)
    (rows,) = call(gather_kernel, [VM], [(ALL, LOW)], "gather")(over_yx(parts))
    res1, packed = call(middle_kernel, [SM] + [VM] * 6, [(TOK, SHARE), (2 * ALL, LOW)], "middle")(
        core, over_z(rows), cotangent, acts, gates, owners, slots
    )
    (sent,) = call(spread_kernel, [VM], [(NY * NX, 2 * YROWS, LOW)], "spread")(
        over_z(packed)
    )
    parts, *keep, give = call(
        lower_kernel, [SM] + [VM] * 5 + [VM, HB] * 2, [blocks] + [wide] * 4 + [(4,) + wide], "lower",
        [pltpu.VMEM((4,) + wide, BF), pltpu.VMEM((WIDTH, HID), BF), pltpu.VMEM((HID, WIDTH), BF),
         pltpu.SemaphoreType.DMA((4,)), pltpu.SemaphoreType.DMA((2, CUTS))], places=[VM] * 5 + [HB],
    )(core, over_yx(sent), *kept1, *weights)
    came = lax.ppermute(give, "segment", SWAP)
    (rows,) = call(gather_kernel, [VM], [(ALL, LOW)], "gather")(over_yx(parts))

    grad_in, grad_out = call(
        weight_kernel, [HB] * 5, [(WIDTH, HID), (HID, WIDTH)], "weight",
        [pltpu.VMEM((4, 2 * NY * NZ * CAP, WIDTH), BF), pltpu.VMEM((2, WIDTH, HID), BF), pltpu.SemaphoreType.DMA((10,))],
        mib=56, cost=(2 * 10**9, 6 * 10**6), places=[HB, HB],
    )(*keep, came)
    mine, other, grad_in = call(
        end_kernel, [SM] + [VM] * 4 + [HB], [(TOK, SHARE)] * 2 + [(WIDTH, HID)], "end",
        places=[VM, VM, HB], alias={5: 2},
    )(core, over_z(rows), res1, owners, slots, grad_in)
    got = lax.ppermute(other, "segment", SWAP)
    grads = jnp.stack([jnp.where(top, got, mine), jnp.where(top, mine, got)])
    return grads[None], grad_in[None, None], grad_out[None, None]


def solution(mesh):
    fine = Mesh(mesh.devices.reshape(2, NY, NZ, NX), ("segment", "y", "z", "pair"))
    e = ("y", "z")
    placed = (
        P(None, None, e, "pair"),
        P(None, e, "pair"),
        P(None, None, e),
        P(None, None, e),
        P(None, None, e),
        P("segment", e, None, "pair"),
        P("segment", e, "pair", None),
    )
    return jax.shard_map(
        body,
        mesh=fine,
        in_specs=placed,
        out_specs=(
            P("segment", None, e, "pair"),
            P("segment", e, None, "pair"),
            P("segment", e, "pair", None),
        ),
        check_vma=False,
    )
```

```python
import functools

import jax
import jax.numpy as jnp
from jax import lax
from jax.experimental import pallas as pl
from jax.experimental.pallas import tpu as pltpu
from jax.sharding import Mesh, PartitionSpec as P

BF = jnp.bfloat16
F32 = jnp.float32
I32 = jnp.int32
SWAP = [(0, 1), (1, 0)]

NY, NZ, NX = 4, 16, 4
CAP = 4
TOK = 192
SHARE = 192
WIDTH = SHARE * NX
FIRST = NZ // 2
HID = 768
LOW = 128
ZROWS = NY * CAP + NY * CAP // 2
YROWS = NZ * CAP + NZ * CAP // 2
CUTS = 4
ALL = NZ * ZROWS


def dot(a, b, ca=1, cb=0):
    return lax.dot_general(a, b, (((ca,), (cb,)), ((), ())), preferred_element_type=F32)


def hot(cond):
    return jnp.where(cond, 1.0, 0.0).astype(BF)


def iota(shape, dim):
    return lax.broadcasted_iota(I32, shape, dim)


def column(row):
    n = row.shape[1]
    eye = iota((n, n), 0) == iota((n, n), 1)
    return jnp.sum(jnp.where(eye, row.astype(F32), 0.0), axis=1, keepdims=True)


def targets(owner, slot):
    base = ((owner + FIRST) & (NZ - 1)) * ZROWS
    y = owner >> 4
    return base + y * CAP + slot, base + NY * CAP + y * 2 + (slot >> 1), slot & 1


def routes(owner, slot):
    low_at, high_at, odd = targets(owner, slot)
    at = iota((ALL, TOK), 0)
    low = hot(at == low_at)
    even_hot = hot((at == high_at) & (odd == 0))
    odd_hot = hot((at == high_at) & (odd == 1))
    return low, even_hot, odd_hot


def pack(values, hots):
    low, even_hot, odd_hot = hots
    out = []
    for v in values:
        high = v[:, LOW:]
        none = jnp.zeros_like(high)
        out.append(
            dot(low, v[:, :LOW])
            + dot(even_hot, jnp.concatenate([high, none], axis=1))
            + dot(odd_hot, jnp.concatenate([none, high], axis=1))
        )
    return out


def unpack(rows, owner, slot):
    low_at, high_at, odd = (column(t).astype(I32) for t in targets(owner, slot))
    at = iota((TOK, ALL), 1)
    low = dot(hot(at == low_at), rows)
    even_rows = dot(hot((at == high_at) & (odd == 0)), rows)
    odd_rows = dot(hot((at == high_at) & (odd == 1)), rows)
    high = even_rows[:, : SHARE - LOW] + odd_rows[:, SHARE - LOW :]
    return jnp.concatenate([low, high], axis=1)


def row_of(ref, layer, core):
    return jnp.where(core == 0, ref[layer, 0:1, :], ref[layer, 1:2, :])


def joined(parts):
    parts = [p.reshape(NZ, ZROWS, LOW) for p in parts]
    return jnp.concatenate(parts, axis=1).reshape(len(parts) * ALL, LOW).astype(BF)


def start_kernel(core_ref, acts, cot, gates, owners, slots, out, tok, gate_v, owner_v, slot_v, sems):
    core = core_ref[0]
    copies = [
        pltpu.make_async_copy(src, dst, sems.at[k])
        for k, (src, dst) in enumerate(
            [
                (owners, owner_v),
                (slots, slot_v),
                (gates, gate_v),
                (cot.at[core], tok.at[0]),
                (acts.at[1, core], tok.at[1]),
            ]
        )
    ]
    for copy in copies:
        copy.start()
    copies[0].wait()
    copies[1].wait()
    upper = routes(row_of(owner_v, 1, core), row_of(slot_v, 1, core))
    for copy in copies[2:]:
        copy.wait()
    gate = column(row_of(gate_v, 1, core))
    scaled = (gate * tok[0].astype(F32)).astype(BF)
    first = pack([tok[1], scaled], upper)
    out[...] = joined(first)


def spread_move():
    shape = (NY, YROWS, ALL)
    y, k, at = iota(shape, 0), iota(shape, 1), iota(shape, 2)
    z = (k & 31) >> 1
    half = k & 1
    low = z * ZROWS + y * CAP + half * 2 + (k >> 5)
    high = z * ZROWS + NY * CAP + y * 2 + half
    return hot((at == jnp.where(k < NZ * CAP, low, high)).reshape(ALL, ALL))


def moved_parts(rows):
    move = spread_move()
    value = rows[...].astype(F32).reshape(NZ, 2 * ZROWS, LOW)
    for a in range(2):
        part = value[:, a * ZROWS : (a + 1) * ZROWS].reshape(ALL, LOW).astype(BF)
        yield a, dot(move, part).astype(BF)


def spread_kernel(rows, out):
    for a, moved in moved_parts(rows):
        for j in range(NY):
            for i in range(NX):
                out[j * NX + i, a * YROWS : (a + 1) * YROWS, :] = moved[j * YROWS : (j + 1) * YROWS]


def gather_kernel(parts, out):
    shape = (NZ, ZROWS, ALL)
    z, k, at = iota(shape, 0), iota(shape, 1), iota(shape, 2)
    low = (k >> 2) * YROWS + (k & 1) * 32 + z * 2 + ((k & 3) >> 1)
    k2 = k - NY * CAP
    high = (k2 >> 1) * YROWS + NZ * CAP + z * 2 + (k2 & 1)
    move = hot((at == jnp.where(k < NY * CAP, low, high)).reshape(ALL, ALL))
    sums = []
    for j in range(NY):
        total = parts[j * NX].astype(F32)
        for i in range(1, NX):
            total = total + parts[j * NX + i].astype(F32)
        sums.append(total)
    out[...] = dot(move, jnp.concatenate(sums, axis=0).astype(BF)).astype(BF)


def assemble(ref, first):
    rows = []
    for j in range(NY):
        cols = []
        for i in range(NX):
            low = ref[j * NX + i, first : first + 64, :]
            high = ref[j * NX + i, first + 64 : first + YROWS, :]
            cols.append(low)
            cols.append(jnp.concatenate([high[:, :64], high[:, 64:]], axis=0))
        rows.append(jnp.concatenate(cols, axis=1))
    return jnp.concatenate(rows, axis=0)


def expert_step(x, grad, w_in, w_out, out, save):
    save(3, grad)
    inv = lax.rsqrt(jnp.mean(x * x, axis=1, keepdims=True) + 1e-06)
    normed = (x * inv).astype(BF)
    save(0, normed)
    u = dot(normed, w_in())
    square = u * u
    s = jnp.tanh(0.7978845608 * (u + 0.044715 * square * u))
    save(2, (0.5 * u * (1.0 + s)).astype(BF))
    slope = 0.5 * (1.0 + s) + 0.5 * u * (1.0 - s * s) * 0.7978845608 * (1.0 + 0.134145 * square)
    back = (dot(grad, w_out(), 1, 1) * slope).astype(BF)
    save(1, back)
    part = dot(back, w_in(), 1, 1)
    inner = jnp.sum(part * x, axis=1, keepdims=True)
    branch = (inv * part - (inv * inv * inv * inner * (1.0 / WIDTH)) * x).astype(BF)
    for j in range(NY):
        for i in range(NX):
            at = i * SHARE
            block = branch[j * 64 : (j + 1) * 64]
            out[j * NX + i, 0:64, :] = block[:, at : at + LOW]
            out[j * NX + i, 64:YROWS, :] = jnp.concatenate(
                [block[:32, at + LOW : at + SHARE], block[32:, at + LOW : at + SHARE]], axis=1
            )


def held(ref):
    return lambda: ref[...]


def fetched(source, buffer, sems):
    step = WIDTH // CUTS
    copies = [
        pltpu.make_async_copy(source.at[k * step : (k + 1) * step], buffer.at[k * step : (k + 1) * step], sems.at[k])
        for k in range(CUTS)
    ]
    for copy in copies:
        copy.start()

    def value():
        while copies:
            copies.pop(0).wait()
        return buffer[...]

    return value


def upper_kernel(core_ref, saved, own_in, other_in, own_out, other_out, out, k0, k1, k2, k3, in_buf, out_buf, sems):
    def run(w_in, w_out):
        def save(k, value):
            (k0, k1, k2, k3)[k][...] = value

        expert_step(assemble(saved, 0).astype(F32), assemble(saved, YROWS), w_in, w_out, out, save)

    @pl.when(core_ref[0] == 1)
    def _():
        run(held(own_in), held(own_out))

    @pl.when(core_ref[0] != 1)
    def _():
        run(fetched(other_in, in_buf, sems.at[0]), fetched(other_out, out_buf, sems.at[1]))


def lower_kernel(
    core_ref, saved, n1, b1, h1, g1, own_in, other_in, own_out, other_out,
    out, k0, k1, k2, k3, give, kept, in_buf, out_buf, sems, more,
):
    keep, above = (k0, k1, k2, k3), (n1, b1, h1, g1)

    def run(w_in, w_out, save):
        expert_step(assemble(saved, 0).astype(F32), assemble(saved, YROWS), w_in, w_out, out, save)

    @pl.when(core_ref[0] == 0)
    def _():
        copies = [pltpu.make_async_copy(above[k], give.at[k], sems.at[k]) for k in range(4)]
        for copy in copies:
            copy.start()

        def save(k, value):
            keep[k][...] = value

        run(held(own_in), held(own_out), save)
        for copy in copies:
            copy.wait()

    @pl.when(core_ref[0] != 0)
    def _():
        w_in, w_out = fetched(other_in, in_buf, more.at[0]), fetched(other_out, out_buf, more.at[1])
        copies = [pltpu.make_async_copy(kept.at[k], give.at[k], sems.at[k]) for k in range(4)]

        def save(k, value):
            kept[k] = value
            copies[k].start()
            keep[k][...] = above[k][...]

        run(w_in, w_out, save)
        for copy in copies:
            copy.wait()


def weight_kernel(k0, k1, k2, k3, came, first, second, rows, sums, sems):
    half = NY * NZ * CAP
    loads = [
        [pltpu.make_async_copy(src, rows.at[k, n * half : (n + 1) * half], sems.at[2 * k + n])
         for n, src in enumerate([(k0, k1, k2, k3)[k], came.at[k]])]
        for k in range(4)
    ]
    for pair in loads:
        for copy in pair:
            copy.start()

    def product(k, at, dst):
        for copy in loads[k] + loads[k + 1]:
            copy.wait()
        sums[at] = dot(rows[k], rows[k + 1], 0, 0).astype(BF)
        copy = pltpu.make_async_copy(sums.at[at], dst, sems.at[8 + at])
        copy.start()
        return copy

    stores = [product(0, 0, first), product(2, 1, second)]
    for copy in stores:
        copy.wait()


def middle_kernel(core_ref, rows, cot, acts, gates, owners, slots, result, out):
    core = core_ref[0]
    branch = unpack(rows[...], row_of(owners, 1, core), row_of(slots, 1, core))
    res = (cot[core].astype(F32) + branch).astype(BF)
    result[...] = res
    gate = column(row_of(gates, 0, core))
    scaled = (gate * res.astype(F32)).astype(BF)
    out[...] = joined(pack([acts[0, core], scaled], routes(row_of(owners, 0, core), row_of(slots, 0, core))))


def end_kernel(core_ref, rows, above, owners, slots, grad_in, keep, give, same):
    core = core_ref[0]
    branch = unpack(rows[...], row_of(owners, 0, core), row_of(slots, 0, core))
    res = (above[...].astype(F32) + branch).astype(BF)
    keep[...] = jnp.where(core == 0, res, above[...])
    give[...] = jnp.where(core == 0, above[...], res)


VM = pl.BlockSpec(memory_space=pltpu.VMEM)
SM = pl.BlockSpec(memory_space=pltpu.SMEM)
HB = pl.BlockSpec(memory_space=pltpu.HBM)


def call(kernel, ins, outs, name, scratch=(), mib=16, cost=None, places=None, alias=None):
    return pl.pallas_call(
        kernel,
        in_specs=list(ins),
        out_specs=places or [VM] * len(outs),
        out_shape=[o if hasattr(o, "dtype") else jax.ShapeDtypeStruct(o, BF) for o in outs],
        scratch_shapes=list(scratch),
        compiler_params=pltpu.CompilerParams(vmem_limit_bytes=mib << 20),
        cost_estimate=cost and pl.CostEstimate(flops=cost[0], bytes_accessed=cost[1], transcendentals=0),
        input_output_aliases=alias or {},
        name=name,
    )


def over_z(x):
    ring = [[(FIRST + k) % NZ for k in range(NZ)]]
    x = x.reshape(NZ, -1, LOW)
    return lax.all_to_all(x, "z", 0, 0, axis_index_groups=ring, tiled=True).reshape(-1, LOW)


def over_yx(x):
    return lax.all_to_all(x, ("y", "pair"), 0, 0, tiled=True)


def body(acts, cotangent, gates, owners, slots, w_in, w_out):
    index = lax.axis_index("segment")
    top = index == 1
    core = index.astype(I32).reshape(1)
    own_in, own_out = w_in[0, 0], w_out[0, 0]
    other_in = lax.ppermute(own_in, "segment", SWAP)
    other_out = lax.ppermute(own_out, "segment", SWAP)
    weights = (own_in, other_in, own_out, other_out)

    table = (2, 2, TOK)
    (packed,) = call(
        start_kernel, [SM] + [HB] * 5, [(2 * ALL, LOW)], "start",
        [pltpu.VMEM((2, TOK, SHARE), BF), pltpu.VMEM(table, F32), pltpu.VMEM(table, I32),
         pltpu.VMEM(table, I32), pltpu.SemaphoreType.DMA((6,))], mib=60,
    )(core, acts, cotangent, gates, owners, slots)
    (sent,) = call(spread_kernel, [VM], [(NY * NX, 2 * YROWS, LOW)], "spread", mib=62)(
        over_z(packed)
    )
    saved = over_yx(sent)
    blocks, wide = (NY * NX, YROWS, LOW), (NY * NZ * CAP, WIDTH)
    parts, *kept1 = call(
        upper_kernel, [SM, VM] + [VM, HB] * 2, [blocks] + [wide] * 4, "upper",
        [pltpu.VMEM((WIDTH, HID), BF), pltpu.VMEM((HID, WIDTH), BF), pltpu.SemaphoreType.DMA((2, CUTS))],
    )(core, saved, *weights)
    (rows,) = call(gather_kernel, [VM], [(ALL, LOW)], "gather")(over_yx(parts))
    res1, packed = call(middle_kernel, [SM] + [VM] * 6, [(TOK, SHARE), (2 * ALL, LOW)], "middle")(
        core, over_z(rows), cotangent, acts, gates, owners, slots
    )
    (sent,) = call(spread_kernel, [VM], [(NY * NX, 2 * YROWS, LOW)], "spread")(
        over_z(packed)
    )
    parts, *keep, give = call(
        lower_kernel, [SM] + [VM] * 5 + [VM, HB] * 2, [blocks] + [wide] * 4 + [(4,) + wide], "lower",
        [pltpu.VMEM((4,) + wide, BF), pltpu.VMEM((WIDTH, HID), BF), pltpu.VMEM((HID, WIDTH), BF),
         pltpu.SemaphoreType.DMA((4,)), pltpu.SemaphoreType.DMA((2, CUTS))], places=[VM] * 5 + [HB],
    )(core, over_yx(sent), *kept1, *weights)
    came = lax.ppermute(give, "segment", SWAP)
    (rows,) = call(gather_kernel, [VM], [(ALL, LOW)], "gather")(over_yx(parts))

    grad_in, grad_out = call(
        weight_kernel, [HB] * 5, [(WIDTH, HID), (HID, WIDTH)], "weight",
        [pltpu.VMEM((4, 2 * NY * NZ * CAP, WIDTH), BF), pltpu.VMEM((2, WIDTH, HID), BF), pltpu.SemaphoreType.DMA((10,))],
        mib=56, cost=(2 * 10**9, 6 * 10**6), places=[HB, HB],
    )(*keep, came)
    mine, other, grad_in = call(
        end_kernel, [SM] + [VM] * 4 + [HB], [(TOK, SHARE)] * 2 + [(WIDTH, HID)], "end",
        places=[VM, VM, HB], alias={5: 2},
    )(core, over_z(rows), res1, owners, slots, grad_in)
    got = lax.ppermute(other, "segment", SWAP)
    grads = jnp.stack([jnp.where(top, got, mine), jnp.where(top, mine, got)])
    return grads[None], grad_in[None, None], grad_out[None, None]


def solution(mesh):
    fine = Mesh(mesh.devices.reshape(2, NY, NZ, NX), ("segment", "y", "z", "pair"))
    e = ("y", "z")
    placed = (
        P(None, None, e, "pair"),
        P(None, e, "pair"),
        P(None, None, e),
        P(None, None, e),
        P(None, None, e),
        P("segment", e, None, "pair"),
        P("segment", e, "pair", None),
    )
    return jax.shard_map(
        body,
        mesh=fine,
        in_specs=placed,
        out_specs=(
            P("segment", None, e, "pair"),
            P("segment", e, None, "pair"),
            P("segment", e, "pair", None),
        ),
        check_vma=False,
    )
```
